32 devices in a mesh: wide: 8 (over y, x, core), narrow: 4 (over z).
Axes of the slice: x: 2, y: 2, z: 4, core: 2. Of those that a mesh axis runs over, the one named last changes fastest.
Arguments:
- hidden_in: bfloat16 [8192, 2048], P(('wide', 'narrow')), may hold values from -6 to 6
- attn_gain: float32 [2048], replicated, may hold values from 0.5 to 1.5
- mlp_gain: float32 [2048], replicated, may hold values from 0.5 to 1.5
- w_query: bfloat16 [2048, 2048], P(None, 'narrow'), may hold values from -0.125 to 0.125
- w_key: bfloat16 [2048, 512], P(None, 'narrow'), may hold values from -0.125 to 0.125
- w_value: bfloat16 [2048, 512], P(None, 'narrow'), may hold values from -0.125 to 0.125
- w_out: bfloat16 [2048, 2048], P('narrow'), may hold values from -0.5 to 0.5
- w_gate: bfloat16 [2048, 8192], P(None, 'narrow'), may hold values from -0.125 to 0.125
- w_up: bfloat16 [2048, 8192], P(None, 'narrow'), may hold values from -0.125 to 0.125
- w_down: bfloat16 [8192, 2048], P('narrow'), may hold values from -0.0625 to 0.0625
- upstream: bfloat16 [8192, 2048], P(('wide', 'narrow')), may hold values from -6 to 6
- doc_lengths: int32 [8, 4], P('wide'), may hold values from 1 to 896, as said below
Outputs:
- layer_out: bfloat16 [8192, 2048], P(('wide', 'narrow'))
- input_grad: float32 [8192, 2048], P(('wide', 'narrow'))
- attn_gain_grad: float32 [2048], replicated
- mlp_gain_grad: float32 [2048], replicated
- query_grad: float32 [2048, 2048], P('wide', 'narrow')
- key_grad: float32 [2048, 512], P('wide', 'narrow')
- value_grad: float32 [2048, 512], P('wide', 'narrow')
- out_proj_grad: float32 [2048, 2048], P('narrow', 'wide')
- gate_grad: float32 [2048, 8192], P('wide', 'narrow')
- up_grad: float32 [2048, 8192], P('wide', 'narrow')
- down_grad: float32 [8192, 2048], P('narrow', 'wide')
The draws below stay inside these ranges and needn't reach their ends.
Inputs may be any that keep to these rules, and one draw needn't show every extreme that they name: `doc_lengths`: in every group one document has 896 tokens and the other 3 have 256 // 2 tokens together; the lengths of a group sum to 1024.
All inputs are finite; a program needn't handle non-finite values.
Results may differ from the reference program's by a relative error of at most 0.018.
Values may be sent and summed in bfloat16 or wider, within the bound.
No kernel may reach another device: no remote copies, remote signals or barrier semaphores. Data moves between devices by JAX's collectives and lax.ppermute only.
A program may use at most 256 MiB of HBM per device.

```python
import math
import jax
import jax.numpy as jnp
from jax import lax

D = 2048
H = 32
KV = 8
HD = 64
FF = 8192
GROUP_TOK = 1024
DOCS = 4
TOK_DEV = 256
TOKENS = 8192
N_WIDE = 8


def draw_doc_lengths(key, part):
    key = jax.random.fold_in(key, 7)
    short_total = TOK_DEV // 2
    long_length = GROUP_TOK - short_total

    def one_group(group_key):
        cut_key, place_key = jax.random.split(group_key)
        cuts = jnp.sort(jax.random.permutation(cut_key, short_total - 1)[:DOCS - 2] + 1).astype(jnp.int32)
        bounds = jnp.concatenate([jnp.zeros((1,), jnp.int32), cuts, jnp.full((1,), short_total, jnp.int32)])
        shorts = bounds[1:] - bounds[:-1]
        place = jax.random.randint(place_key, (), 0, DOCS)
        indices = jnp.arange(DOCS, dtype=jnp.int32)
        source_index = jnp.clip(indices - (indices > place).astype(jnp.int32), 0, DOCS - 2)
        return jnp.where(indices == place, long_length, shorts[source_index]).astype(jnp.int32)
    return jax.vmap(one_group)(jax.random.split(key, N_WIDE))


def spiked(values, rng, source, target, parts, factor):
    def block_of(axis_at):
        return (jnp.arange(values.shape[axis_at]) // (values.shape[axis_at] // parts)).reshape((-1,) + (1,) * (values.ndim - 1 - axis_at))

    first = jax.random.permutation(rng, parts)[block_of(target)]
    far = (block_of(target) + parts // 2) % parts
    return jnp.where((block_of(source) == first) | (block_of(source) == far), factor * values, values)


def levels(rng, extent, cuts, least, largest):
    def one(dim, blocks):
        heights = jax.random.uniform(jax.random.fold_in(jax.random.fold_in(rng, 6), dim), (blocks,), jnp.float32, least / len(cuts), largest / len(cuts))
        return jnp.repeat(jnp.exp(heights), extent[dim] // blocks).reshape((-1,) + (1,) * (len(extent) - dim - 1))

    loudness = one(*cuts[0])
    for cut in cuts[1:]:
        loudness = loudness * one(*cut)
    return loudness


def centred(rng, extent, spread, limit, cuts=(), held_as=jnp.bfloat16):
    loudness = levels(rng, extent, cuts, -0.22, 0.18) if cuts else 1.0
    values = jax.random.normal(rng, extent, jnp.float32) * spread * loudness
    return jnp.minimum(jnp.maximum(values, -limit), limit).astype(held_as)


def gaussian_with(stream_key, extent, spread, reach, shards, heavy, held_as=jnp.bfloat16):
    entries = spread * jax.random.normal(stream_key, extent, jnp.float32)
    if shards:
        entries = entries * levels(stream_key, extent, shards, -0.22, 0.18)
    return jnp.clip(spiked(entries, jax.random.fold_in(stream_key, 3), *heavy), -reach, reach).astype(held_as)


def setup_inputs(seed: int = 0) -> dict:
    arg_keys = jax.random.split(jax.random.key(seed), 13)
    hidden_in = centred(arg_keys[0], (TOKENS, D), 1.0, 6.0, ((0, 32),))
    attn_gain = jnp.clip(1.0 + 0.1 * jax.random.normal(arg_keys[1], (D,), jnp.float32), 0.5, 1.5)
    mlp_gain = jnp.clip(1.0 + 0.1 * jax.random.normal(arg_keys[2], (D,), jnp.float32), 0.5, 1.5)
    w_query = centred(arg_keys[3], (D, H * HD), D ** -0.5, 0.125, ((1, 4),))
    w_key = centred(arg_keys[4], (D, KV * HD), D ** -0.5, 0.125, ((1, 4),))
    w_value = centred(arg_keys[5], (D, KV * HD), D ** -0.5, 0.125, ((1, 4),))
    w_out = centred(arg_keys[6], (H * HD, D), (H * HD // 16) ** -0.5, 0.5, ((0, 4),))
    w_gate = centred(arg_keys[7], (D, FF), D ** -0.5, 0.125, ((1, 4),))
    w_up = centred(arg_keys[8], (D, FF), D ** -0.5, 0.125, ((1, 4),))
    w_down = centred(arg_keys[9], (FF, D), FF ** -0.5, 0.0625, ((0, 4),))
    upstream = gaussian_with(arg_keys[10], (TOKENS, D), 1.0, 6.0, ((0, 32),), (0, 1, 32, 2.75))
    doc_lengths = draw_doc_lengths(jax.random.fold_in(arg_keys[12], 71), 0)
    return dict(hidden_in=hidden_in, attn_gain=attn_gain, mlp_gain=mlp_gain, w_query=w_query, w_key=w_key, w_value=w_value, w_out=w_out, w_gate=w_gate, w_up=w_up, w_down=w_down, upstream=upstream, doc_lengths=doc_lengths)


EPSILON = 1e-05
THETA_BASE = 500000.0

@jax.custom_vjp
def low(v):
    return lax.optimization_barrier(v.astype(jnp.bfloat16)).astype(jnp.float32)

@jax.custom_vjp
def low_back(v):
    return v

def low_keep(v):
    return (low(v), None)

def low_pass(kept, grad):
    return (grad,)

def back_keep(v):
    return (v, None)

def back_low(kept, grad):
    return (low(grad),)
low.defvjp(low_keep, low_pass)
low_back.defvjp(back_keep, back_low)

def doc_layout(lengths, total_rows):
    lengths = lengths.astype(jnp.int32)
    ends = jnp.cumsum(lengths).astype(jnp.int32)
    starts = (ends - lengths).astype(jnp.int32)
    places = jnp.arange(total_rows, dtype=jnp.int32)
    owner = lax.optimization_barrier(jnp.sum((places[:, None] >= ends[None, :]).astype(jnp.int32), axis=1)).astype(jnp.int32)
    picked = owner[:, None] == jnp.arange(lengths.shape[0], dtype=jnp.int32)[None, :]
    first = lax.optimization_barrier(jnp.sum(jnp.where(picked, starts[None, :], 0), axis=1)).astype(jnp.int32)
    return (owner, (places - first).astype(jnp.float32))

def angle_tables(positions, head_size):
    indices = jnp.arange(head_size // 2, dtype=jnp.float32)
    inverse = jnp.exp(indices * (-2.0 * math.log(THETA_BASE) / head_size))
    turned = positions[:, None] * inverse[None, :]
    return (jnp.cos(turned), jnp.sin(turned))

def rotate(values, cosine, sine):
    half = values.shape[-1] // 2
    first, second = (values[..., :half], values[..., half:])
    cosine = cosine[:, None, :]
    sine = sine[:, None, :]
    return jnp.concatenate([first * cosine - second * sine, second * cosine + first * sine], axis=-1)

def rms_scale(values, gain):
    return values * lax.rsqrt(lax.optimization_barrier(jnp.mean(values * values, axis=-1, keepdims=True)) + EPSILON) * gain

def layer(hidden, gain_one, gain_two, weights, owner, positions):
    w_query, w_key, w_value, w_out, w_gate, w_up, w_down = weights
    highest = lax.Precision.HIGHEST
    total_rows = hidden.shape[0]
    group = H // KV
    normed = low(rms_scale(hidden, gain_one))
    query_raw = low_back(jnp.dot(normed, w_query, precision=highest))
    key_raw = low_back(jnp.dot(normed, w_key, precision=highest))
    value_all = low(low_back(jnp.dot(normed, w_value, precision=highest))).reshape(total_rows, KV, HD)
    cosine, sine = angle_tables(positions, HD)
    queries = low(rotate(query_raw.reshape(total_rows, H, HD), cosine, sine)).reshape(total_rows, KV, group, HD)
    keys = low(rotate(key_raw.reshape(total_rows, KV, HD), cosine, sine))
    block = min(512, total_rows)
    count = total_rows // block
    scale = HD ** (-0.5)

    def attend(query_block, first_row, keys, value_all, owner):
        columns = jnp.arange(total_rows, dtype=jnp.int32)
        scores = low_back(jnp.einsum('qcgd,kcd->cgqk', query_block, keys, precision=highest) * scale)
        row_ids = first_row + jnp.arange(block, dtype=jnp.int32)
        row_owner = lax.dynamic_slice_in_dim(owner, first_row, block)
        allowed = (row_owner[:, None] == owner[None, :]) & (columns[None, :] <= row_ids[:, None])
        weights_soft = jax.nn.softmax(jnp.where(allowed, scores, -1e+30), axis=-1)
        return jnp.einsum('cgqk,kcd->qcgd', low(weights_soft), value_all, precision=highest)
    checked = jax.checkpoint(attend)
    blocks = queries.reshape(count, block, KV, group, HD)
    firsts = jnp.arange(count, dtype=jnp.int32) * block
    attended = lax.map(lambda element: checked(element[0], element[1], keys, value_all, owner), (blocks, firsts))
    heads_out = low(low_back(attended.reshape(total_rows, H * HD)))
    branch = low_back(jnp.dot(heads_out, w_out, precision=highest))
    resid = hidden + branch
    normed_two = low(rms_scale(resid, gain_two))
    gate = low_back(jnp.dot(normed_two, w_gate, precision=highest))
    up_value = low_back(jnp.dot(normed_two, w_up, precision=highest))
    product = low(jax.nn.silu(gate) * up_value)
    return resid + jnp.dot(product, w_down, precision=highest)

def reference(hidden_in, attn_gain, mlp_gain, w_query, w_key, w_value, w_out, w_gate, w_up, w_down, upstream, doc_lengths):
    weights = tuple((matrix.astype(jnp.float32) for matrix in (w_query, w_key, w_value, w_out, w_gate, w_up, w_down)))
    inputs = hidden_in.astype(jnp.float32).reshape(N_WIDE, GROUP_TOK, D)
    grads_in = upstream.astype(jnp.float32).reshape(N_WIDE, GROUP_TOK, D)

    def one_group(sums, element):
        group_in, group_grad, lengths = element
        owner, positions = doc_layout(lengths, GROUP_TOK)

        def forward(hidden, gain_one, gain_two, *mats):
            return layer(hidden, gain_one, gain_two, mats, owner, positions)
        result, pullback = jax.vjp(forward, group_in, attn_gain, mlp_gain, *weights)
        grads = pullback(group_grad)
        sums = tuple((running + part for running, part in zip(sums, grads[1:])))
        return (sums, (result.astype(jnp.bfloat16), grads[0]))
    zeros = tuple((jnp.zeros(array.shape, jnp.float32) for array in (attn_gain, mlp_gain) + weights))
    sums, (outputs, input_grads) = lax.scan(one_group, zeros, (inputs, grads_in, doc_lengths))
    return (outputs.reshape(TOKENS, D), input_grads.reshape(TOKENS, D), sums[0], sums[1], sums[2], sums[3], sums[4], sums[5], sums[6], sums[7], sums[8])
```

```python
import functools, math
import jax, jax.numpy as jnp
from jax import lax
from jax.experimental import pallas as pl
from jax.experimental.pallas import tpu as pltpu

from jax.sharding import PartitionSpec as P

HD = 64
EPSILON = 1e-05
THETA_BASE = 500000.0
LANES = 128
VMEM_LIMIT = 56 * 1024 * 1024


def dot_nn(a, b):
    return lax.dot_general(a, b, (((1,), (0,)), ((), ())), preferred_element_type=jnp.float32)


def dot_nt(a, b):
    return lax.dot_general(a, b, (((1,), (1,)), ((), ())), preferred_element_type=jnp.float32)


def swap_halves(x):
    parts = []
    for t in range(x.shape[1] // LANES):
        tile = x[:, t * LANES : (t + 1) * LANES]
        lane = lax.broadcasted_iota(jnp.int32, tile.shape, 1)
        left = pltpu.roll(tile, LANES - HD // 2, 1)
        right = pltpu.roll(tile, HD // 2, 1)
        parts.append(jnp.where(lane % HD < HD // 2, left, right))
    return parts[0] if len(parts) == 1 else jnp.concatenate(parts, axis=1)


def turn(x, cosine, sine):
    n = x.shape[1] // LANES
    s = swap_halves(x)
    outs = [
        x[:, i * LANES : (i + 1) * LANES] * cosine + s[:, i * LANES : (i + 1) * LANES] * sine
        for i in range(n)
    ]
    return outs[0] if n == 1 else jnp.concatenate(outs, axis=1)


def qkv_body(qw, kw, x_ref, w_ref, cos_ref, sin_ref, q_ref, k_ref, v_ref):
    y = dot_nn(x_ref[...], w_ref[...])
    c, s = cos_ref[...], sin_ref[...]
    q_ref[...] = (turn(y[:, :qw], c, s) * (HD ** -0.5)).astype(jnp.bfloat16)
    k_ref[...] = turn(y[:, qw : qw + kw], c, s).astype(jnp.bfloat16)
    v_ref[...] = y[:, qw + kw :].astype(jnp.bfloat16)


def qkv_call(x, w, cosine, sine, qw, kw):
    rows, d = x.shape
    br = min(256, rows)
    spec = lambda n: pl.BlockSpec((br, n), lambda i: (i, 0))
    return pl.pallas_call(
        functools.partial(qkv_body, qw, kw),
        grid=(rows // br,),
        in_specs=[spec(d), pl.BlockSpec(w.shape, lambda i: (0, 0)), spec(LANES), spec(LANES)],
        out_specs=[spec(qw), spec(kw), spec(kw)],
        out_shape=[
            jax.ShapeDtypeStruct((rows, qw), jnp.bfloat16),
            jax.ShapeDtypeStruct((rows, kw), jnp.bfloat16),
            jax.ShapeDtypeStruct((rows, kw), jnp.bfloat16),
        ],
        compiler_params=pltpu.CompilerParams(vmem_limit_bytes=VMEM_LIMIT),
        cost_estimate=pl.CostEstimate(
            flops=2 * rows * d * w.shape[1], bytes_accessed=2 * (x.size + w.size) + 4 * rows * qw, transcendentals=0
        ),
        name="qkv",
    )(x, w, cosine, sine)


def half_mask(rows):
    lane = lax.broadcasted_iota(jnp.int32, (rows, LANES), 1)
    return lane < HD


def stack_heads(x, low):
    zero = jnp.zeros((x.shape[0], LANES), x.dtype)
    a, b = x[:, :LANES], x[:, LANES : 2 * LANES]
    return jnp.concatenate(
        [jnp.where(low, a, zero), jnp.where(low, zero, a), jnp.where(low, b, zero), jnp.where(low, zero, b)], axis=0
    )


def unstack_heads(x, low):
    r = x.shape[0] // 4
    return jnp.concatenate(
        [jnp.where(low, x[:r], x[r : 2 * r]), jnp.where(low, x[2 * r : 3 * r], x[3 * r :])], axis=1
    )


def allowed_mask(ext, b0, r, start):
    j = lax.broadcasted_iota(jnp.int32, (ext, 4 * r), 0)
    t = lax.broadcasted_iota(jnp.int32, (ext, 4 * r), 1) % r + b0
    return (j <= t) & (j >= start)


def block_extent(b0, r, total):
    return min(total, -(-(b0 + r) // LANES) * LANES)


def fwd_body(blocks, r, kv, group, q_ref, k_ref, v_ref, start_ref, o_ref, lse_ref):
    low = half_mask(r)
    total = k_ref.shape[0]
    width = group * HD
    for c in range(kv):
        vt = v_ref[:, c * LANES : (c + 1) * LANES].T
        for n, b0 in enumerate(blocks):
            ext = block_extent(b0, r, total)
            q4 = stack_heads(q_ref[b0 : b0 + r, c * width : (c + 1) * width], low)
            s = dot_nt(k_ref[:ext, c * LANES : (c + 1) * LANES], q4)
            s = jnp.where(allowed_mask(ext, b0, r, start_ref[n : n + 1, :]), s, -1e30)
            top = jnp.max(s, axis=0, keepdims=True)
            p = jnp.exp(s - top)
            total_p = jnp.sum(p, axis=0, keepdims=True)
            ot = dot_nn(vt[:, :ext], p.astype(jnp.bfloat16)) * (1.0 / total_p)
            o_ref[n * r : (n + 1) * r, c * width : (c + 1) * width] = unstack_heads(ot.T, low).astype(jnp.bfloat16)
            lse_ref[c, n : n + 1, :] = top + jnp.log(total_p)


def attend(q, k, v, start, blocks, r, kv, group):
    nb = len(blocks)
    area = sum(block_extent(b, r, q.shape[0]) for b in blocks) * r * kv * group
    return pl.pallas_call(
        functools.partial(fwd_body, blocks, r, kv, group),
        out_shape=[
            jax.ShapeDtypeStruct((nb * r, kv * group * HD), jnp.bfloat16),
            jax.ShapeDtypeStruct((kv, nb, 4 * r), jnp.float32),
        ],
        compiler_params=pltpu.CompilerParams(vmem_limit_bytes=VMEM_LIMIT),
        cost_estimate=pl.CostEstimate(flops=area * 512, bytes_accessed=4 << 20, transcendentals=area),
        name="attend",
    )(q, k, v, start)


def bwd_body(blocks, r, kv, group, first, last, *refs):
    refs = list(refs)
    q_ref, k_ref, v_ref, start_ref, do_ref, o_ref, lse_ref = refs[:7]
    refs = refs[7:]
    if not first:
        dq_in, dk_in, dv_in = refs[:3]
        refs = refs[3:]
    if last:
        cos_ref, sin_ref = refs[:2]
        out_ref, dq_s, dk_s, dv_s = refs[2:]
    else:
        dq_s, dk_s, dv_s = refs
    low = half_mask(r)
    total = k_ref.shape[0]
    width = group * HD
    for c in range(kv):
        cl = slice(c * LANES, (c + 1) * LANES)
        cw = slice(c * width, (c + 1) * width)
        kt = k_ref[:, cl].T
        if first:
            dk_s[:, cl] = jnp.zeros((total, LANES), jnp.float32)
            dv_s[:, cl] = jnp.zeros((total, LANES), jnp.float32)
        else:
            dk_s[:, cl] = dk_in[:, cl]
            dv_s[:, cl] = dv_in[:, cl]
        for n, b0 in enumerate(blocks):
            ext = block_extent(b0, r, total)
            q4 = stack_heads(q_ref[b0 : b0 + r, cw], low)
            do4 = stack_heads(do_ref[n * r : (n + 1) * r, cw], low)
            o4 = stack_heads(o_ref[n * r : (n + 1) * r, cw], low)
            delta = jnp.sum((do4.astype(jnp.float32) * o4.astype(jnp.float32)).T, axis=0, keepdims=True)
            s = dot_nt(k_ref[:ext, cl], q4)
            p = jnp.exp(
                jnp.where(allowed_mask(ext, b0, r, start_ref[n : n + 1, :]), s - lse_ref[c, n : n + 1, :], -1e30)
            )
            dp = dot_nt(v_ref[:ext, cl], do4)
            ds = (p * (dp - delta)).astype(jnp.bfloat16)
            dq4 = dot_nn(kt[:, :ext], ds).T
            dq_s[n * r : (n + 1) * r, cw] = unstack_heads(dq4, low) * (HD ** -0.5)
            dk_s[:ext, cl] += dot_nn(ds, q4)
            dv_s[:ext, cl] += dot_nn(p.astype(jnp.bfloat16), do4)
    if not last:
        return
    nc = 1 if first else 2
    cosine, sine = cos_ref[...], -sin_ref[...]
    qw = kv * width
    for n, b0 in enumerate(blocks):
        cs, sn = cos_ref[b0 : b0 + r, :], -sin_ref[b0 : b0 + r, :]
        out_ref[b0 : b0 + r, :qw] = turn(dq_s[n * r : (n + 1) * r, :], cs, sn).astype(jnp.bfloat16)
        if not first:
            a0 = b0 - r
            cs, sn = cos_ref[a0 : a0 + r, :], -sin_ref[a0 : a0 + r, :]
            out_ref[a0 : a0 + r, :qw] = turn(dq_in[n * r : (n + 1) * r, :], cs, sn).astype(jnp.bfloat16)
    lane = lax.broadcasted_iota(jnp.int32, (total, LANES), 1) < HD

    def fold(x):
        return x + pltpu.roll(x, HD, 1)

    for i, (ref, rot) in enumerate(((dk_s, True), (dv_s, False))):
        for c in range(0, kv, 2):
            x = fold(ref[:, c * LANES : (c + 1) * LANES])
            if c + 1 < kv:
                x = jnp.where(lane, x, fold(ref[:, (c + 1) * LANES : (c + 2) * LANES]))
            if rot:
                x = turn(x, cosine, sine)
            x = x.astype(jnp.bfloat16)
            at = qw + i * kv * HD + c * HD
            if c + 1 < kv:
                out_ref[:, at : at + LANES] = x
            else:
                out_ref[:, at : at + HD] = x[:, :HD]


def attend_back(q, k, v, start, do, o, lse, carried, tables, blocks, r, kv, group):
    first, last = carried is None, tables is not None
    rows = q.shape[0]
    nb = len(blocks)
    area = sum(block_extent(b, r, rows) for b in blocks) * r * kv * group
    sums = [
        jax.ShapeDtypeStruct((nb * r, kv * group * HD), jnp.float32),
        jax.ShapeDtypeStruct((rows, kv * LANES), jnp.float32),
        jax.ShapeDtypeStruct((rows, kv * LANES), jnp.float32),
    ]
    if last:
        out = jax.ShapeDtypeStruct((rows, kv * (group + 2) * HD), jnp.bfloat16)
        scratch = [pltpu.VMEM(s.shape, s.dtype) for s in sums]
    else:
        out, scratch = sums, []
    args = (q, k, v, start, do, o, lse) + (() if first else tuple(carried)) + (tuple(tables) if last else ())
    return pl.pallas_call(
        functools.partial(bwd_body, blocks, r, kv, group, first, last),
        out_shape=out,
        scratch_shapes=scratch,
        compiler_params=pltpu.CompilerParams(vmem_limit_bytes=VMEM_LIMIT),
        cost_estimate=pl.CostEstimate(flops=area * 1280, bytes_accessed=8 << 20, transcendentals=area),
        name="attend_back",
    )(*args)


def mlp_body(x_ref, dy_ref, wg_ref, wu_ref, wd_ref, m_ref, dg_ref, du_ref):
    x = x_ref[...]
    dy = dy_ref[...].reshape(x.shape)
    gate = dot_nn(x, wg_ref[...])
    up = dot_nn(x, wu_ref[...])
    dm = dot_nt(dy, wd_ref[...])
    sig = 1.0 / (1.0 + jnp.exp(-gate))
    act = gate * sig
    m_ref[...] = (act * up).astype(jnp.bfloat16)
    du_ref[...] = (dm * act).astype(jnp.bfloat16)
    dg_ref[...] = (dm * up * (sig * (1.0 + gate * (1.0 - sig)))).astype(jnp.bfloat16)


def mlp_call(x, dy, wg, wu, wd):
    t, d = x.shape
    f = wg.shape[1]
    bf = min(256, f)
    col = pl.BlockSpec((d, bf), lambda i: (0, i))
    out = pl.BlockSpec((t, bf), lambda i: (0, i))
    res = pl.BlockSpec((t, d), lambda i: (0, 0))
    return pl.pallas_call(
        mlp_body,
        grid=(f // bf,),
        in_specs=[res, res, col, col, pl.BlockSpec((bf, d), lambda i: (i, 0))],
        out_specs=[out] * 3,
        out_shape=[jax.ShapeDtypeStruct((t, f), jnp.bfloat16)] * 3,
        compiler_params=pltpu.CompilerParams(vmem_limit_bytes=VMEM_LIMIT),
        cost_estimate=pl.CostEstimate(flops=6 * t * d * f, bytes_accessed=2 * (2 * x.size + 3 * wg.size + 3 * t * f), transcendentals=t * f),
        name="mlp",
    )(x, dy, wg, wu, wd)


def grad_body(nl, nr, got, tiles_ref, *refs):
    lefts = refs[:nl]
    rights = [refs[nl + i * nl : nl + (i + 1) * nl] for i in range(nr)]
    refs = refs[nl + nl * nr :]
    recvs, outs = (refs[:nr], refs[nr:]) if got else ([None] * nr, refs)
    turned = [x[...].T for x in lefts]
    for right, recv, out in zip(rights, recvs, outs):
        total = dot_nn(turned[0], right[0][...])
        for a, b in zip(turned[1:], right[1:]):
            total += dot_nn(a, b[...])
        if got:
            total += recv[0].astype(jnp.float32)
        out[0] = total.astype(jnp.bfloat16)


def grad_call(tiles, part, lefts, rights, recvs=()):
    count = tiles.shape[0]
    nl, nr = len(lefts), len(rights)
    outs = [jax.ShapeDtypeStruct((count, part, r[0].shape[1]), jnp.bfloat16) for r in rights]
    out_specs = [pl.BlockSpec((1, part, r[0].shape[1]), lambda j, t: (j, 0, 0)) for r in rights]
    in_specs = [pl.BlockSpec((x.shape[0], part), lambda j, t: (0, t[j])) for x in lefts]
    in_specs += [
        pl.BlockSpec(x.shape, lambda j, t: (0, 0), pipeline_mode=pl.Buffered(1)) for r in rights for x in r
    ]
    if recvs:
        in_specs += out_specs
    rows = sum(x.shape[0] for x in lefts)
    cols = sum(r[0].shape[1] for r in rights)
    return pl.pallas_call(
        functools.partial(grad_body, nl, nr, bool(recvs)),
        grid_spec=pltpu.PrefetchScalarGridSpec(
            num_scalar_prefetch=1, grid=(count,), in_specs=in_specs, out_specs=out_specs
        ),
        out_shape=outs,
        compiler_params=pltpu.CompilerParams(vmem_limit_bytes=VMEM_LIMIT),
        cost_estimate=pl.CostEstimate(
            flops=2 * rows * count * part * cols,
            bytes_accessed=2 * (rows * (count * part + cols) + count * part * cols * (2 if recvs else 1)),
            transcendentals=0,
        ),
        name="weight_grad",
    )(tiles, *lefts, *[x for r in rights for x in r], *recvs)


def doc_layout(lengths, total_rows):
    ends = jnp.cumsum(lengths)
    starts = ends - lengths
    places = jnp.arange(total_rows, dtype=jnp.int32)
    owner = jnp.sum((places[:, None] >= ends[None, :]).astype(jnp.int32), axis=1)
    picked = owner[:, None] == jnp.arange(lengths.shape[0], dtype=jnp.int32)[None, :]
    first = jnp.sum(jnp.where(picked, starts[None, :], 0), axis=1)
    return first, (places - first).astype(jnp.float32)


def angle_tables(positions):
    indices = jnp.arange(HD // 2, dtype=jnp.float32)
    inverse = jnp.exp(indices * (-2.0 * math.log(THETA_BASE) / HD))
    turned = positions[:, None] * inverse[None, :]
    cosine, sine = jnp.cos(turned), jnp.sin(turned)
    return (
        jnp.concatenate([cosine] * 4, axis=1),
        jnp.concatenate([-sine, sine, -sine, sine], axis=1),
    )


def twice(w):
    heads = w.shape[1] // HD
    return jnp.concatenate([w[:, i * HD : (i + 1) * HD] for i in range(heads) for _ in range(2)], axis=1)


def after(value, *others):
    return lax.optimization_barrier((value, *others))[0]


def scatter_direct(parts, index, size):
    def block(at):
        return lax.dynamic_index_in_dim(parts, at, 0, keepdims=False)

    total = block(index).astype(jnp.float32)
    for k in range(1, size):
        got = lax.ppermute(block(index ^ k), "narrow", [(i, i ^ k) for i in range(size)])
        total = total + got.astype(jnp.float32)
    return total


def gather_line(block, index, size):
    rows = block.shape[0]
    up, down = [], []
    a = b = block
    for step in range(1, size):
        a = lax.ppermute(a, "narrow", [(i, i + 1) for i in range(step - 1, size - 1)])
        b = lax.ppermute(b, "narrow", [(i, i - 1) for i in range(1, size - step + 1)])
        up.append(a)
        down.append(b)
    full = jnp.zeros((size * rows, block.shape[1]), block.dtype)
    full = lax.dynamic_update_slice_in_dim(full, block, index * rows, 0)
    for k in range(1, size):
        got = jnp.where(index >= k, up[k - 1], down[size - k - 1])
        full = lax.dynamic_update_slice_in_dim(full, got, lax.rem(index + size - k, size) * rows, 0)
    return full


def scatter_narrow(parts, size):
    return lax.psum_scatter(
        parts.reshape(-1, parts.shape[-1]), "narrow", scatter_dimension=0, tiled=True
    ).astype(jnp.float32)


def wide_grads(lefts, rights, order, index, size):
    bits = size.bit_length() - 1
    part = lefts[0].shape[1] // size
    mine = index & 1
    pairs = 2 * jnp.arange(size // 2, dtype=jnp.int32)
    sent = grad_call(pairs + (1 - mine), part, lefts, rights)
    got = [lax.ppermute(x, "wide", [(i, i ^ 1) for i in range(size)]) for x in sent]
    sums = grad_call(pairs + mine, part, lefts, rights, got)
    results = []
    for value, bit_order in zip(sums, order):
        value = value.reshape((2,) * (bits - 1) + value.shape[1:])
        left = list(range(1, bits))[::-1]
        for bit in bit_order:
            axis = left.index(bit)
            left.pop(axis)
            here = (index >> bit) & 1
            out = lax.dynamic_index_in_dim(value, 1 - here, axis, keepdims=False).astype(jnp.bfloat16)
            kept = lax.dynamic_index_in_dim(value, here, axis, keepdims=False)
            got = lax.ppermute(out, "wide", [(i, i ^ (1 << bit)) for i in range(size)])
            value = kept.astype(jnp.float32) + got.astype(jnp.float32)
        results.append(value)
    return results


def sum_all(array, wide, narrow):
    for axis, size in (("wide", wide), ("narrow", narrow)):
        step = 1
        while step < size:
            array = array + lax.ppermute(array, axis, [(i, i ^ step) for i in range(size)])
            step *= 2
    return array


def on_device(
    hidden_in, attn_gain, mlp_gain, w_query, w_key, w_value, w_out, w_gate, w_up, w_down, upstream, doc_lengths
):
    narrow, wide = lax.axis_size("narrow"), lax.axis_size("wide")
    here, wide_here = lax.axis_index("narrow"), lax.axis_index("wide")
    local_rows, width = hidden_in.shape
    total_rows = local_rows * narrow
    chunks = 2
    r = local_rows // chunks
    query_width, key_width = w_query.shape[1], w_key.shape[1]
    kv = key_width // HD
    group = query_width // key_width
    first, positions = doc_layout(doc_lengths[0], total_rows)
    tables = angle_tables(positions)
    first_rows = first.astype(jnp.int32).reshape(narrow, chunks, r)
    starts = [jnp.tile(first_rows[:, c], (1, 4)) for c in range(chunks)]
    blocks = [[z * local_rows + c * r for z in range(narrow)] for c in range(chunks)]
    w_twice = jnp.concatenate([w_query, twice(w_key), twice(w_value)], axis=1)
    w_joined = jnp.concatenate([w_query, w_key, w_value], axis=1)

    source = hidden_in.astype(jnp.float32)
    inverse_one = lax.rsqrt(jnp.mean(source * source, axis=-1, keepdims=True) + EPSILON)
    unit_one = source * inverse_one
    normed_one = (unit_one * attn_gain).astype(jnp.bfloat16)
    full_one = lax.all_gather(normed_one, "narrow", axis=0, tiled=True)
    q, k, v = qkv_call(full_one, w_twice, *tables, query_width, 2 * key_width)

    def rows_of(array, c):
        return array[c * r : (c + 1) * r]

    def out_parts(o):
        parts = jnp.dot(o, w_out, preferred_element_type=jnp.float32).astype(jnp.bfloat16)
        return parts.reshape(narrow, r, width)

    def second_norm(c, summed):
        resid = rows_of(source, c) + summed
        inverse = lax.rsqrt(jnp.mean(resid * resid, axis=-1, keepdims=True) + EPSILON)
        unit = resid * inverse
        return resid, inverse, unit, (unit * mlp_gain).astype(jnp.bfloat16)

    heads_a, lse_a = attend(q, k, v, starts[0], blocks[0], r, kv, group)
    parts_a = out_parts(heads_a)
    summed_a = scatter_narrow(parts_a, narrow)
    q_late, upstream_late, _ = lax.optimization_barrier((q, upstream, parts_a))
    dy_full = gather_line(upstream_late, here, narrow).reshape(narrow, chunks, r, width)
    heads_b, lse_b = attend(q_late, k, v, starts[1], blocks[1], r, kv, group)
    summed_b = scatter_direct(out_parts(heads_b), here, narrow)
    resid_a, inverse_a, unit_a, normed_a = second_norm(0, summed_a)
    full_a = lax.all_gather(normed_a, "narrow", axis=0, tiled=True)
    resid_b, inverse_b, unit_b, normed_b = second_norm(1, summed_b)
    normed_b = after(normed_b, normed_a)
    full_b = lax.all_gather(normed_b, "narrow", axis=0, tiled=True)
    dy_a, dy_b = (dy_full[:, c].reshape(narrow * r, width) for c in range(chunks))

    def mlp_back(dg, du):
        return (dot_nt(dg, w_gate) + dot_nt(du, w_up)).astype(jnp.bfloat16).reshape(narrow, r, width)

    def second_back(c, grad, unit, inverse):
        scaled = grad * mlp_gain
        back = rows_of(upstream, c).astype(jnp.float32) + inverse * (
            scaled - unit * jnp.mean(scaled * unit, axis=-1, keepdims=True)
        )
        return back, jnp.sum(grad * unit, axis=0)

    m_a, dg_a, du_a = mlp_call(full_a, dy_a, w_gate, w_up, w_down)
    parts_a = mlp_back(dg_a, du_a)
    grad_a = scatter_narrow(parts_a, narrow)
    full_b = after(full_b, parts_a)
    m_b, dg_b, du_b = mlp_call(full_b, dy_b, w_gate, w_up, w_down)
    parts_b = mlp_back(dg_b, du_b)
    grad_b = scatter_direct(parts_b, here, narrow)
    back_a, gain_two_a = second_back(0, grad_a, unit_a, inverse_a)
    back_b, gain_two_b = second_back(1, grad_b, unit_b, inverse_b)
    low_a, low_b = back_a.astype(jnp.bfloat16), back_b.astype(jnp.bfloat16)
    back_full_a = lax.all_gather(low_a, "narrow", axis=0, tiled=True)
    back_full_b = lax.all_gather(after(low_b, low_a), "narrow", axis=0, tiled=True)

    m_a, m_b, dg_a, dg_b, du_a, du_b, _ = lax.optimization_barrier((m_a, m_b, dg_a, dg_b, du_a, du_b, parts_b))
    high = list(range(1, wide.bit_length() - 1))
    swap = high[::-1]
    gate_sum, up_sum = wide_grads(
        [full_a, full_b], [[dg_a, dg_b], [du_a, du_b]], [high, swap], wide_here, wide
    )
    (down_sum,) = wide_grads([dy_a, dy_b], [[m_a, m_b]], [high], wide_here, wide)

    def layer_rows(m, resid):
        parts = jnp.dot(m, w_down, preferred_element_type=jnp.float32).astype(jnp.bfloat16)
        return (resid + scatter_direct(parts.reshape(narrow, r, width), here, narrow)).astype(jnp.bfloat16)

    layer_out = jnp.concatenate([layer_rows(m_a, resid_a), layer_rows(m_b, resid_b)], axis=0)

    heads_grad_a = dot_nt(back_full_a, w_out).astype(jnp.bfloat16)
    carried = attend_back(
        q, k, v, starts[0], heads_grad_a, heads_a, lse_a, None, None, blocks[0], r, kv, group
    )
    back_full_b = after(back_full_b, carried[0])
    heads_grad_b = dot_nt(back_full_b, w_out).astype(jnp.bfloat16)
    joined_grad = attend_back(
        q, k, v, starts[1], heads_grad_b, heads_b, lse_b, carried, tables, blocks[1], r, kv, group
    )
    parts = dot_nt(joined_grad, w_joined).astype(jnp.bfloat16)
    normed_one_grad = scatter_narrow(parts, narrow)
    parts = after(parts, joined_grad)
    gain_one = jnp.sum(parts.astype(jnp.float32) * full_one.astype(jnp.float32), axis=0) / attn_gain
    gains = sum_all(jnp.stack([gain_one, gain_two_a + gain_two_b]), wide, narrow)
    joined_late = after(joined_grad, parts)
    (joined_sum,) = wide_grads([full_one], [[joined_late]], [high], wide_here, wide)
    (out_sum,) = wide_grads([back_full_a, back_full_b], [[heads_a, heads_b]], [swap], wide_here, wide)
    scaled_one = normed_one_grad * attn_gain
    resid_grad = jnp.concatenate([back_a, back_b], axis=0)
    input_grad = resid_grad + inverse_one * (
        scaled_one - unit_one * jnp.mean(scaled_one * unit_one, axis=-1, keepdims=True)
    )
    return (
        layer_out,
        input_grad,
        gains[0],
        gains[1],
        joined_sum[:, :query_width],
        joined_sum[:, query_width : query_width + key_width],
        joined_sum[:, query_width + key_width :],
        out_sum.T,
        gate_sum,
        up_sum,
        down_sum.T,
    )


def solution(mesh):
    in_specs = (
        P(("wide", "narrow"), None),
        P(),
        P(),
        P(None, "narrow"),
        P(None, "narrow"),
        P(None, "narrow"),
        P("narrow", None),
        P(None, "narrow"),
        P(None, "narrow"),
        P("narrow", None),
        P(("wide", "narrow"), None),
        P("wide", None),
    )
    out_specs = (
        P(("wide", "narrow"), None),
        P(("wide", "narrow"), None),
        P(),
        P(),
        P("wide", "narrow"),
        P("wide", "narrow"),
        P("wide", "narrow"),
        P("narrow", "wide"),
        P("wide", "narrow"),
        P("wide", "narrow"),
        P("narrow", "wide"),
    )
    return jax.shard_map(
        on_device, mesh=mesh, in_specs=in_specs, out_specs=out_specs, check_vma=False
    )
```

```python
import functools, math
import jax, jax.numpy as jnp
from jax import lax
from jax.experimental import pallas as pl
from jax.experimental.pallas import tpu as pltpu

from jax.sharding import PartitionSpec as P

HD = 64
EPSILON = 1e-05
THETA_BASE = 500000.0
LANES = 128
VMEM_LIMIT = 56 * 1024 * 1024
COST = pl.CostEstimate(flops=1, bytes_accessed=1, transcendentals=0)


def dot_nn(a, b):
    return lax.dot_general(a, b, (((1,), (0,)), ((), ())), preferred_element_type=jnp.float32)


def dot_nt(a, b):
    return lax.dot_general(a, b, (((1,), (1,)), ((), ())), preferred_element_type=jnp.float32)


def swap_halves(x):
    parts = []
    for t in range(x.shape[1] // LANES):
        tile = x[:, t * LANES : (t + 1) * LANES]
        lane = lax.broadcasted_iota(jnp.int32, tile.shape, 1)
        left = pltpu.roll(tile, LANES - HD // 2, 1)
        right = pltpu.roll(tile, HD // 2, 1)
        parts.append(jnp.where(lane % HD < HD // 2, left, right))
    return parts[0] if len(parts) == 1 else jnp.concatenate(parts, axis=1)


def turn(x, cosine, sine):
    n = x.shape[1] // LANES
    s = swap_halves(x)
    outs = [
        x[:, i * LANES : (i + 1) * LANES] * cosine + s[:, i * LANES : (i + 1) * LANES] * sine
        for i in range(n)
    ]
    return outs[0] if n == 1 else jnp.concatenate(outs, axis=1)


def qkv_body(qw, kw, x_ref, w_ref, cos_ref, sin_ref, q_ref, k_ref, v_ref):
    y = dot_nn(x_ref[...], w_ref[...])
    c, s = cos_ref[...], sin_ref[...]
    q_ref[...] = (turn(y[:, :qw], c, s) * (HD ** -0.5)).astype(jnp.bfloat16)
    k_ref[...] = turn(y[:, qw : qw + kw], c, s).astype(jnp.bfloat16)
    v_ref[...] = y[:, qw + kw :].astype(jnp.bfloat16)


def qkv_call(x, w, cosine, sine, qw, kw):
    rows, d = x.shape
    br = min(256, rows)
    spec = lambda n: pl.BlockSpec((br, n), lambda i: (i, 0))
    return pl.pallas_call(
        functools.partial(qkv_body, qw, kw),
        grid=(rows // br,),
        in_specs=[spec(d), pl.BlockSpec(w.shape, lambda i: (0, 0)), spec(LANES), spec(LANES)],
        out_specs=[spec(qw), spec(kw), spec(kw)],
        out_shape=[
            jax.ShapeDtypeStruct((rows, qw), jnp.bfloat16),
            jax.ShapeDtypeStruct((rows, kw), jnp.bfloat16),
            jax.ShapeDtypeStruct((rows, kw), jnp.bfloat16),
        ],
        compiler_params=pltpu.CompilerParams(vmem_limit_bytes=VMEM_LIMIT),
        cost_estimate=COST,
        name="qkv",
    )(x, w, cosine, sine)


def half_mask(rows):
    lane = lax.broadcasted_iota(jnp.int32, (rows, LANES), 1)
    return lane < HD


def stack_heads(x, low):
    zero = jnp.zeros((x.shape[0], LANES), x.dtype)
    a, b = x[:, :LANES], x[:, LANES : 2 * LANES]
    return jnp.concatenate(
        [jnp.where(low, a, zero), jnp.where(low, zero, a), jnp.where(low, b, zero), jnp.where(low, zero, b)], axis=0
    )


def unstack_heads(x, low):
    r = x.shape[0] // 4
    return jnp.concatenate(
        [jnp.where(low, x[:r], x[r : 2 * r]), jnp.where(low, x[2 * r : 3 * r], x[3 * r :])], axis=1
    )


def allowed_mask(ext, b0, r, start):
    j = lax.broadcasted_iota(jnp.int32, (ext, 4 * r), 0)
    t = lax.broadcasted_iota(jnp.int32, (ext, 4 * r), 1) % r + b0
    return (j <= t) & (j >= start)


def block_extent(b0, r, total):
    return min(total, -(-(b0 + r) // LANES) * LANES)


def fwd_body(blocks, r, kv, group, q_ref, k_ref, v_ref, start_ref, o_ref, lse_ref):
    low = half_mask(r)
    total = k_ref.shape[0]
    width = group * HD
    for c in range(kv):
        vt = v_ref[:, c * LANES : (c + 1) * LANES].T
        for n, b0 in enumerate(blocks):
            ext = block_extent(b0, r, total)
            q4 = stack_heads(q_ref[b0 : b0 + r, c * width : (c + 1) * width], low)
            s = dot_nt(k_ref[:ext, c * LANES : (c + 1) * LANES], q4)
            s = jnp.where(allowed_mask(ext, b0, r, start_ref[n : n + 1, :]), s, -1e30)
            top = jnp.max(s, axis=0, keepdims=True)
            p = jnp.exp(s - top)
            total_p = jnp.sum(p, axis=0, keepdims=True)
            ot = dot_nn(vt[:, :ext], p.astype(jnp.bfloat16)) * (1.0 / total_p)
            o_ref[n * r : (n + 1) * r, c * width : (c + 1) * width] = unstack_heads(ot.T, low).astype(jnp.bfloat16)
            lse_ref[c, n : n + 1, :] = top + jnp.log(total_p)


def attend(q, k, v, start, blocks, r, kv, group):
    nb = len(blocks)
    return pl.pallas_call(
        functools.partial(fwd_body, blocks, r, kv, group),
        out_shape=[
            jax.ShapeDtypeStruct((nb * r, kv * group * HD), jnp.bfloat16),
            jax.ShapeDtypeStruct((kv, nb, 4 * r), jnp.float32),
        ],
        compiler_params=pltpu.CompilerParams(vmem_limit_bytes=VMEM_LIMIT),
        cost_estimate=COST,
        name="attend",
    )(q, k, v, start)


def bwd_body(blocks, r, kv, group, first, last, *refs):
    refs = list(refs)
    q_ref, k_ref, v_ref, start_ref, do_ref, o_ref, lse_ref = refs[:7]
    refs = refs[7:]
    if not first:
        dq_in, dk_in, dv_in = refs[:3]
        refs = refs[3:]
    if last:
        cos_ref, sin_ref = refs[:2]
        out_ref, dq_s, dk_s, dv_s = refs[2:]
    else:
        dq_s, dk_s, dv_s = refs
    low = half_mask(r)
    total = k_ref.shape[0]
    width = group * HD
    for c in range(kv):
        cl = slice(c * LANES, (c + 1) * LANES)
        cw = slice(c * width, (c + 1) * width)
        kt = k_ref[:, cl].T
        if first:
            dk_s[:, cl] = jnp.zeros((total, LANES), jnp.float32)
            dv_s[:, cl] = jnp.zeros((total, LANES), jnp.float32)
        else:
            dk_s[:, cl] = dk_in[:, cl]
            dv_s[:, cl] = dv_in[:, cl]
        for n, b0 in enumerate(blocks):
            ext = block_extent(b0, r, total)
            q4 = stack_heads(q_ref[b0 : b0 + r, cw], low)
            do4 = stack_heads(do_ref[n * r : (n + 1) * r, cw], low)
            o4 = stack_heads(o_ref[n * r : (n + 1) * r, cw], low)
            delta = jnp.sum((do4.astype(jnp.float32) * o4.astype(jnp.float32)).T, axis=0, keepdims=True)
            s = dot_nt(k_ref[:ext, cl], q4)
            p = jnp.exp(
                jnp.where(allowed_mask(ext, b0, r, start_ref[n : n + 1, :]), s - lse_ref[c, n : n + 1, :], -1e30)
            )
            dp = dot_nt(v_ref[:ext, cl], do4)
            ds = (p * (dp - delta)).astype(jnp.bfloat16)
            dq4 = dot_nn(kt[:, :ext], ds).T
            dq_s[n * r : (n + 1) * r, cw] = unstack_heads(dq4, low) * (HD ** -0.5)
            dk_s[:ext, cl] += dot_nn(ds, q4)
            dv_s[:ext, cl] += dot_nn(p.astype(jnp.bfloat16), do4)
    if not last:
        return
    nc = 1 if first else 2
    cosine, sine = cos_ref[...], -sin_ref[...]
    qw = kv * width
    for n, b0 in enumerate(blocks):
        cs, sn = cos_ref[b0 : b0 + r, :], -sin_ref[b0 : b0 + r, :]
        out_ref[b0 : b0 + r, :qw] = turn(dq_s[n * r : (n + 1) * r, :], cs, sn).astype(jnp.bfloat16)
        if not first:
            a0 = b0 - r
            cs, sn = cos_ref[a0 : a0 + r, :], -sin_ref[a0 : a0 + r, :]
            out_ref[a0 : a0 + r, :qw] = turn(dq_in[n * r : (n + 1) * r, :], cs, sn).astype(jnp.bfloat16)
    lane = lax.broadcasted_iota(jnp.int32, (total, LANES), 1) < HD

    def fold(x):
        return x + pltpu.roll(x, HD, 1)

    for i, (ref, rot) in enumerate(((dk_s, True), (dv_s, False))):
        for c in range(0, kv, 2):
            x = fold(ref[:, c * LANES : (c + 1) * LANES])
            if c + 1 < kv:
                x = jnp.where(lane, x, fold(ref[:, (c + 1) * LANES : (c + 2) * LANES]))
            if rot:
                x = turn(x, cosine, sine)
            x = x.astype(jnp.bfloat16)
            at = qw + i * kv * HD + c * HD
            if c + 1 < kv:
                out_ref[:, at : at + LANES] = x
            else:
                out_ref[:, at : at + HD] = x[:, :HD]


def attend_back(q, k, v, start, do, o, lse, carried, tables, blocks, r, kv, group):
    first, last = carried is None, tables is not None
    rows = q.shape[0]
    nb = len(blocks)
    sums = [
        jax.ShapeDtypeStruct((nb * r, kv * group * HD), jnp.float32),
        jax.ShapeDtypeStruct((rows, kv * LANES), jnp.float32),
        jax.ShapeDtypeStruct((rows, kv * LANES), jnp.float32),
    ]
    if last:
        out = jax.ShapeDtypeStruct((rows, kv * (group + 2) * HD), jnp.bfloat16)
        scratch = [pltpu.VMEM(s.shape, s.dtype) for s in sums]
    else:
        out, scratch = sums, []
    args = (q, k, v, start, do, o, lse) + (() if first else tuple(carried)) + (tuple(tables) if last else ())
    return pl.pallas_call(
        functools.partial(bwd_body, blocks, r, kv, group, first, last),
        out_shape=out,
        scratch_shapes=scratch,
        compiler_params=pltpu.CompilerParams(vmem_limit_bytes=VMEM_LIMIT),
        cost_estimate=COST,
        name="attend_back",
    )(*args)


def grad_body(nl, nr, got, tiles_ref, *refs):
    lefts = refs[:nl]
    rights = [refs[nl + i * nl : nl + (i + 1) * nl] for i in range(nr)]
    refs = refs[nl + nl * nr :]
    recv, outs = (refs[0], refs[1:]) if got else (None, refs)
    half = pl.num_programs(0) // 2
    step = pl.program_id(0)
    turned = [x[...].T for x in lefts]
    at = 0
    for right in rights:
        total = dot_nn(turned[0], right[0][...])
        for a, b in zip(turned[1:], right[1:]):
            total += dot_nn(a, b[...])
        here = slice(at, at + total.shape[1])
        at += total.shape[1]
        if not got:
            outs[0][0, :, here] = total.astype(jnp.bfloat16)
            continue
        total = (total + recv[0, :, here].astype(jnp.float32)).astype(jnp.bfloat16)

        @pl.when(step < half)
        def _():
            outs[0][0, :, here] = total

        @pl.when(step >= half)
        def _():
            outs[1][0, :, here] = total


def grad_call(tiles, part, lefts, rights, recv=None):
    count = tiles.shape[0]
    half = count // 2
    nl, nr = len(lefts), len(rights)
    cols = sum(r[0].shape[1] for r in rights)
    got = recv is not None
    shift = half if got else 0
    in_specs = [pl.BlockSpec((x.shape[0], part), lambda j, t: (0, t[lax.rem(j + shift, count)])) for x in lefts]
    in_specs += [
        pl.BlockSpec(x.shape, lambda j, t: (0, 0), pipeline_mode=pl.Buffered(1)) for r in rights for x in r
    ]
    if got:
        in_specs.append(pl.BlockSpec((1, part, cols), lambda j, t: (lax.rem(j + shift, count), 0, 0)))
        out_specs = [
            pl.BlockSpec((1, part, cols), lambda j, t: (jnp.minimum(j, half - 1), 0, 0)),
            pl.BlockSpec((1, part, cols), lambda j, t: (jnp.maximum(j - half, 0), 0, 0)),
        ]
        out_shape = [jax.ShapeDtypeStruct((half, part, cols), jnp.bfloat16)] * 2
    else:
        out_specs = pl.BlockSpec((1, part, cols), lambda j, t: (j, 0, 0))
        out_shape = jax.ShapeDtypeStruct((count, part, cols), jnp.bfloat16)
    return pl.pallas_call(
        functools.partial(grad_body, nl, nr, got),
        grid_spec=pltpu.PrefetchScalarGridSpec(
            num_scalar_prefetch=1, grid=(count,), in_specs=in_specs, out_specs=out_specs
        ),
        out_shape=out_shape,
        compiler_params=pltpu.CompilerParams(vmem_limit_bytes=VMEM_LIMIT),
        cost_estimate=COST,
        name="weight_grad",
    )(tiles, *lefts, *[x for r in rights for x in r], *((recv,) if got else ()))


def place(index, part):
    return pl.ds(pl.multiple_of(index * part, part), part)


def out_body(at_ref, x_ref, *refs):
    pieces, out = refs[:-1], refs[-1]
    x = jnp.concatenate([x_ref[j] for j in range(x_ref.shape[0])], axis=1)
    for n, piece in enumerate(pieces):
        out[:, place(at_ref[n], piece.shape[1])] = dot_nn(x, piece[...])


def out_project(at, x, pieces):
    rows, width = x.shape[1], len(pieces) * pieces[0].shape[1]
    return pl.pallas_call(
        out_body,
        in_specs=[pl.BlockSpec(memory_space=pltpu.SMEM)] + [pl.BlockSpec(memory_space=pltpu.VMEM)] * (1 + len(pieces)),
        out_specs=pl.BlockSpec(memory_space=pltpu.VMEM),
        out_shape=jax.ShapeDtypeStruct((rows, width), jnp.float32),
        compiler_params=pltpu.CompilerParams(vmem_limit_bytes=VMEM_LIMIT),
        cost_estimate=COST,
        name="out_project",
    )(at, x, *pieces)


def out_back_body(at_ref, x_ref, *refs):
    pieces, out = refs[:-1], refs[-1]
    total = None
    for n, piece in enumerate(pieces):
        term = dot_nt(x_ref[:, place(at_ref[n], piece.shape[1])], piece[...])
        total = term if total is None else total + term
    total = total.astype(jnp.bfloat16)
    width = out.shape[2]
    for j in range(out.shape[0]):
        out[j] = total[:, j * width : (j + 1) * width]


def out_project_back(at, x, pieces, parts):
    rows, depth = x.shape[0], pieces[0].shape[0]
    return pl.pallas_call(
        out_back_body,
        in_specs=[pl.BlockSpec(memory_space=pltpu.SMEM)] + [pl.BlockSpec(memory_space=pltpu.VMEM)] * (1 + len(pieces)),
        out_specs=pl.BlockSpec(memory_space=pltpu.VMEM),
        out_shape=jax.ShapeDtypeStruct((parts, rows, depth // parts), jnp.bfloat16),
        compiler_params=pltpu.CompilerParams(vmem_limit_bytes=VMEM_LIMIT),
        cost_estimate=COST,
        name="out_project_back",
    )(at, x, *pieces)


def in_back_body(at_ref, x_ref, *refs):
    pieces, out = refs[:-1], refs[-1]
    x = x_ref[...]
    for n, piece in enumerate(pieces):
        out[:, place(at_ref[n], piece.shape[0])] = dot_nt(x, piece[...])


def in_project_back(at, x, pieces):
    rows, width = x.shape[0], len(pieces) * pieces[0].shape[0]
    return pl.pallas_call(
        in_back_body,
        in_specs=[pl.BlockSpec(memory_space=pltpu.SMEM)] + [pl.BlockSpec(memory_space=pltpu.VMEM)] * (1 + len(pieces)),
        out_specs=pl.BlockSpec(memory_space=pltpu.VMEM),
        out_shape=jax.ShapeDtypeStruct((rows, width), jnp.float32),
        compiler_params=pltpu.CompilerParams(vmem_limit_bytes=VMEM_LIMIT),
        cost_estimate=COST,
        name="in_project_back",
    )(at, x, *pieces)


def mlp_body(x_ref, dy_ref, wg_ref, wu_ref, wd_ref, m_ref, dg_ref, du_ref):
    x, dy = x_ref[...], dy_ref[...]
    gate = dot_nn(x, wg_ref[...])
    up = dot_nn(x, wu_ref[...])
    dm = dot_nt(dy, wd_ref[...])
    sig = 1.0 / (1.0 + jnp.exp(-gate))
    act = gate * sig
    m_ref[...] = (act * up).astype(jnp.bfloat16)
    du_ref[...] = (dm * act).astype(jnp.bfloat16)
    dg_ref[...] = (dm * up * (sig * (1.0 + gate * (1.0 - sig)))).astype(jnp.bfloat16)


def mlp_call(x, dy, wg, wu, wd):
    t, d = x.shape
    f = wg.shape[1]
    bf = min(256, f)
    col = pl.BlockSpec((d, bf), lambda i: (0, i))
    hid = pl.BlockSpec((t, bf), lambda i: (0, i))
    held = pl.BlockSpec((t, d), lambda i: (0, 0), pipeline_mode=pl.Buffered(1))
    return pl.pallas_call(
        mlp_body,
        grid=(f // bf,),
        in_specs=[held, held, col, col, pl.BlockSpec((bf, d), lambda i: (i, 0))],
        out_specs=[hid] * 3,
        out_shape=[jax.ShapeDtypeStruct((t, f), jnp.bfloat16)] * 3,
        compiler_params=pltpu.CompilerParams(vmem_limit_bytes=VMEM_LIMIT),
        cost_estimate=COST,
        name="mlp",
    )(x, dy, wg, wu, wd)


def mlp_back_body(dg_ref, du_ref, wg_ref, wu_ref, o_ref):
    o_ref[...] = (dot_nt(dg_ref[...], wg_ref[...]) + dot_nt(du_ref[...], wu_ref[...])).astype(jnp.bfloat16)


def mlp_back_call(dg, du, wg, wu):
    t, f = dg.shape
    d = wg.shape[0]
    bn = min(256, d)
    held = pl.BlockSpec((t, f), lambda i: (0, 0), pipeline_mode=pl.Buffered(1))
    row = pl.BlockSpec((bn, f), lambda i: (i, 0))
    return pl.pallas_call(
        mlp_back_body,
        grid=(d // bn,),
        in_specs=[held, held, row, row],
        out_specs=pl.BlockSpec((t, bn), lambda i: (0, i)),
        out_shape=jax.ShapeDtypeStruct((t, d), jnp.bfloat16),
        compiler_params=pltpu.CompilerParams(vmem_limit_bytes=VMEM_LIMIT),
        cost_estimate=COST,
        name="mlp_back",
    )(dg, du, wg, wu)


def mat_body(transposed, x_ref, w_ref, o_ref):
    o_ref[...] = (dot_nt if transposed else dot_nn)(x_ref[...], w_ref[...]).astype(jnp.bfloat16)


def mat_call(x, w, transposed):
    rows, depth = x.shape
    width = w.shape[0] if transposed else w.shape[1]
    bn = min(512, width)
    w_spec = pl.BlockSpec((bn, depth), lambda i: (i, 0)) if transposed else pl.BlockSpec((depth, bn), lambda i: (0, i))
    return pl.pallas_call(
        functools.partial(mat_body, transposed),
        grid=(width // bn,),
        in_specs=[pl.BlockSpec((rows, depth), lambda i: (0, 0), pipeline_mode=pl.Buffered(1)), w_spec],
        out_specs=pl.BlockSpec((rows, bn), lambda i: (0, i)),
        out_shape=jax.ShapeDtypeStruct((rows, width), jnp.bfloat16),
        compiler_params=pltpu.CompilerParams(vmem_limit_bytes=VMEM_LIMIT),
        cost_estimate=COST,
        name="product",
    )(x, w)


def down_body(x_ref, w_ref, *refs):
    out = refs[-1]
    out[...] = dot_nn(x_ref[...], w_ref[...]).astype(jnp.bfloat16).reshape(out.shape)


def down_call(x, w, blocks, chunks, chunk, into=None):
    rows, depth = x.shape
    width = w.shape[1]
    bn = min(512, width)
    r = rows // blocks
    return pl.pallas_call(
        down_body,
        grid=(width // bn,),
        in_specs=[
            pl.BlockSpec((rows, depth), lambda i: (0, 0), pipeline_mode=pl.Buffered(1)),
            pl.BlockSpec((depth, bn), lambda i: (0, i)),
        ] + ([] if into is None else [pl.BlockSpec(memory_space=pl.ANY)]),
        out_specs=pl.BlockSpec((blocks, 1, r, bn), lambda i: (0, chunk, 0, i)),
        out_shape=jax.ShapeDtypeStruct((blocks, chunks, r, width), jnp.bfloat16),
        input_output_aliases={} if into is None else {2: 0},
        compiler_params=pltpu.CompilerParams(vmem_limit_bytes=VMEM_LIMIT),
        cost_estimate=COST,
        name="down",
    )(x, w, *(() if into is None else (into,)))


def doc_layout(lengths, total_rows):
    ends = jnp.cumsum(lengths)
    starts = ends - lengths
    places = jnp.arange(total_rows, dtype=jnp.int32)
    owner = jnp.sum((places[:, None] >= ends[None, :]).astype(jnp.int32), axis=1)
    picked = owner[:, None] == jnp.arange(lengths.shape[0], dtype=jnp.int32)[None, :]
    first = jnp.sum(jnp.where(picked, starts[None, :], 0), axis=1)
    return first, (places - first).astype(jnp.float32)


def angle_tables(positions):
    indices = jnp.arange(HD // 2, dtype=jnp.float32)
    inverse = jnp.exp(indices * (-2.0 * math.log(THETA_BASE) / HD))
    turned = positions[:, None] * inverse[None, :]
    cosine, sine = jnp.cos(turned), jnp.sin(turned)
    return (
        jnp.concatenate([cosine] * 4, axis=1),
        jnp.concatenate([-sine, sine, -sine, sine], axis=1),
    )


def twice(w):
    heads = w.shape[1] // HD
    return jnp.concatenate([w[:, i * HD : (i + 1) * HD] for i in range(heads) for _ in range(2)], axis=1)


def after(value, *others):
    return lax.optimization_barrier((value, *others))[0]


def scatter_direct(parts, index, size):
    def block(at):
        return lax.dynamic_index_in_dim(parts, at, 0, keepdims=False)

    total = block(index).astype(jnp.float32)
    for k in range(1, size):
        got = lax.ppermute(block(index ^ k), "narrow", [(i, i ^ k) for i in range(size)])
        total = total + got.astype(jnp.float32)
    return total


def swap_blocks(block, index, size):
    return [block(index)] + [
        lax.ppermute(block(index ^ k), "narrow", [(i, i ^ k) for i in range(size)]) for k in range(1, size)
    ]


def in_order(items, index):
    step = 1
    while step < len(items):
        flip = (index & step) != 0
        items = [jnp.where(flip, items[k ^ step], items[k]) for k in range(len(items))]
        step *= 2
    return items


def high_bits(size):
    first = list(range(1, size.bit_length() - 1))
    return first, first[::-1]


def by_core(size, step):
    bits = high_bits(size)
    return [(i, i ^ (1 << bits[i & 1][step])) for i in range(size)]


def masks(size):
    both = []
    for bits in high_bits(size):
        out = [0]
        for bit in bits[::-1]:
            out = out + [o ^ (1 << bit) for o in out]
        both.append(jnp.array(out, dtype=jnp.int32))
    return both


def gather_plane(piece, size):
    pieces = [piece]
    for step in range(size.bit_length() - 2)[::-1]:
        pieces = pieces + [lax.ppermute(p, "wide", by_core(size, step)) for p in pieces]
    return pieces


def gather_cores(pieces, index, size):
    even, odd = masks(size)
    first = (index & 1) == 0
    pieces = pieces + [lax.ppermute(p, "wide", [(i, i ^ 1) for i in range(size)]) for p in pieces]
    owners = jnp.concatenate([index ^ jnp.where(first, even, odd), index ^ 1 ^ jnp.where(first, odd, even)])
    return pieces, owners.astype(jnp.int32)


def scatter_narrow(parts):
    return lax.psum_scatter(parts, "narrow", scatter_dimension=0, tiled=True)


def grads_sent(lefts, rights, index, size):
    even, odd = masks(size)
    part = lefts[0].shape[1] // size
    tiles = (index ^ 1 ^ jnp.where((index & 1) == 0, odd, even)).astype(jnp.int32)
    return grad_call(tiles, part, lefts, rights)


def swap_cores(sent, size):
    return lax.ppermute(sent, "wide", [(i, i ^ 1) for i in range(size)])


def grads_kept(lefts, rights, got, index, size):
    even, odd = masks(size)
    part = lefts[0].shape[1] // size
    tiles = (index ^ jnp.where((index & 1) == 0, even, odd)).astype(jnp.int32)
    return grad_call(tiles, part, lefts, rights, got)


def swap_plane(sent, step, size):
    return lax.ppermute(sent, "wide", by_core(size, step))


def halve(sent, kept, step, size):
    return kept.astype(jnp.float32) + swap_plane(sent, step, size).astype(jnp.float32)


def halve_again(value, step, size):
    half = value.shape[0] // 2
    return halve(value[half:], value[:half], step, size)


def sum_plane(array, size):
    items = [array] + [
        lax.ppermute(array, "wide", [(i, i ^ (2 * flip)) for i in range(size)]) for flip in range(1, size // 2)
    ]
    return sum(in_order(items, lax.axis_index("wide") >> 1))


def sum_column(array, narrow, size):
    array = array + lax.ppermute(array, "wide", [(i, i ^ 1) for i in range(size)])
    for bit in range(narrow.bit_length() - 1):
        array = array + lax.ppermute(array, "narrow", [(i, i ^ (1 << bit)) for i in range(narrow)])
    return array


def on_device(
    hidden_in, attn_gain, mlp_gain, w_query, w_key, w_value, w_out, w_gate, w_up, w_down, upstream, doc_lengths
):
    narrow, wide = lax.axis_size("narrow"), lax.axis_size("wide")
    here, wide_here = lax.axis_index("narrow"), lax.axis_index("wide")
    local_rows, width = hidden_in.shape
    total_rows = local_rows * narrow
    chunks = 2
    r = local_rows // chunks
    query_width, key_width = w_query.shape[1], w_key.shape[1]
    kv = key_width // HD
    group = query_width // key_width
    first, positions = doc_layout(doc_lengths[0], total_rows)
    tables = angle_tables(positions)
    start = jnp.tile(first.astype(jnp.int32).reshape(narrow, local_rows), (1, 4))
    blocks = [z * local_rows for z in range(narrow)]
    w_twice = jnp.concatenate([w_query, twice(w_key), twice(w_value)], axis=1)
    w_joined = jnp.concatenate([w_query, w_key, w_value], axis=1)
    part = width // wide

    source = hidden_in.astype(jnp.float32)
    inverse_one = lax.rsqrt(jnp.mean(source * source, axis=-1, keepdims=True) + EPSILON)
    unit_one = source * inverse_one
    normed_one = (unit_one * attn_gain).astype(jnp.bfloat16)
    full_one = lax.all_gather(normed_one, "narrow", axis=0, tiled=True)

    w_out_part = lax.dynamic_slice_in_dim(w_out, wide_here * part, part, 1)
    w_out_part = jnp.concatenate(
        in_order(swap_blocks(lambda j: w_out_part, here, narrow), here), axis=0
    )
    w_out_plane = gather_plane(w_out_part, wide)
    full_one, w_twice, tables, w_out_plane = lax.optimization_barrier((full_one, w_twice, tables, w_out_plane))
    w_out_parts, w_out_at = gather_cores(w_out_plane, wide_here, wide)

    dy_a = lax.all_gather(after(upstream[:r], full_one), "narrow", axis=0, tiled=True)
    q, k, v = qkv_call(full_one, w_twice, *tables, query_width, 2 * key_width)

    def swap_heads(x):
        return lax.all_to_all(x.reshape(total_rows, query_width), "narrow", 0, 0, tiled=True)

    def second_norm(summed):
        resid = source + summed
        inverse = lax.rsqrt(jnp.mean(resid * resid, axis=-1, keepdims=True) + EPSILON)
        unit = resid * inverse
        return resid, inverse, unit, (unit * mlp_gain).astype(jnp.bfloat16)

    heads, lse = attend(q, k, v, start, blocks, local_rows, kv, group)
    heads_rows = swap_heads(heads).reshape(narrow, local_rows, query_width)
    dy_b = lax.all_gather(after(upstream[r:], heads_rows), "narrow", axis=0, tiled=True)
    resid, inverse_two, unit_two, normed_two = second_norm(
        out_project(w_out_at, after(heads_rows, dy_a), w_out_parts)
    )
    normed_a, normed_b, dy_b = lax.optimization_barrier((normed_two[:r], normed_two[r:], dy_b))
    full_a = lax.all_gather(normed_a, "narrow", axis=0, tiled=True)
    full_b = lax.all_gather(after(normed_b, full_a), "narrow", axis=0, tiled=True)

    m_a, dg_a, du_a = mlp_call(full_a, dy_a, w_gate, w_up, w_down)
    parts_a = mlp_back_call(dg_a, du_a, w_gate, w_up)
    grad_a = scatter_narrow(parts_a)
    y_a = down_call(after(m_a, parts_a), w_down, narrow, chunks, 0)
    m_b, dg_b, du_b = mlp_call(full_b, after(dy_b, y_a), w_gate, w_up, w_down)
    parts_b = mlp_back_call(dg_b, du_b, w_gate, w_up)
    parts_b, grad_a = lax.optimization_barrier((parts_b, grad_a))
    grad_b = scatter_narrow(parts_b)

    here_wide = (wide_here, wide)
    gate_up = [full_a, after(full_b, parts_b)], [[dg_a, dg_b], [du_a, du_b]]
    sent_gate_up = grads_sent(*gate_up, *here_wide)
    down = [after(dy_a, sent_gate_up), dy_b], [[m_a, m_b]]
    sent_down = grads_sent(*down, *here_wide)
    gate_up = [after(full_a, sent_down), full_b], gate_up[1]
    gate_up_sent, gate_up_kept = grads_kept(*gate_up, swap_cores(sent_gate_up, wide), *here_wide)
    y = down_call(after(m_b, gate_up_sent), w_down, narrow, chunks, 1, y_a)
    layer_sum = lax.psum_scatter(
        after(y, grad_b).reshape(total_rows, width), "narrow", scatter_dimension=0, tiled=True
    )
    unit_late = after(unit_two, y)
    grad_a, grad_b = grad_a.astype(jnp.float32), grad_b.astype(jnp.float32)
    scaled_grad = jnp.concatenate([grad_a, grad_b], axis=0)
    scaled = scaled_grad * mlp_gain
    back = upstream.astype(jnp.float32) + inverse_two * (
        scaled - unit_late * jnp.mean(scaled * unit_late, axis=-1, keepdims=True)
    )
    gain_two = jnp.sum(scaled_grad * unit_late, axis=0)
    low = back.astype(jnp.bfloat16)
    heads_grad = out_project_back(w_out_at, low, w_out_parts, narrow)
    gate_up_kept = after(gate_up_kept, heads_grad)
    heads_side = jnp.concatenate([heads_rows[j] for j in range(narrow)], axis=1)
    out = [after(low, heads_grad)], [[heads_side]]
    sent_out = grads_sent(*out, *here_wide)
    out_sent, out_kept = grads_kept(*out, swap_cores(sent_out, wide), *here_wide)
    gate_up_sum = halve(gate_up_sent, gate_up_kept, 0, wide).astype(jnp.bfloat16)
    rest = gate_up_sum.shape[0] // 2
    gate_up_kept, gate_up_sent = gate_up_sum[:rest], gate_up_sum[rest:]
    heads_grad = swap_heads(heads_grad)
    joined_grad = attend_back(
        after(q, gate_up_sent, out_sent), k, v, start, heads_grad, heads, lse, None, tables, blocks, local_rows, kv,
        group,
    )
    parts = mat_call(joined_grad, after(w_joined, layer_sum), True)
    normed_one_grad = scatter_narrow(parts).astype(jnp.float32)
    gate_up_got = swap_plane(gate_up_sent, 1, wide)
    joined = [after(full_one, parts)], [[joined_grad]]
    sent_joined = grads_sent(*joined, *here_wide)
    parts_late, _ = lax.optimization_barrier((parts, sent_joined))
    gain_one = jnp.sum(parts_late.astype(jnp.float32) * full_one.astype(jnp.float32), axis=0) / attn_gain
    joined = [after(full_one, gain_one)], [[joined_grad]]
    joined_sent, joined_kept = grads_kept(*joined, swap_cores(sent_joined, wide), *here_wide)
    down = [after(dy_a, joined_sent), dy_b], [[m_a, m_b]]
    down_sent, down_kept = grads_kept(*down, swap_cores(sent_down, wide), *here_wide)
    gains = sum_column(sum_plane(after(jnp.stack([gain_one, gain_two]), down_sent), wide), narrow, wide)
    out_sum = halve(out_sent, after(out_kept, parts), 0, wide)
    joined_got = swap_plane(joined_sent, 0, wide)
    down_got = swap_plane(down_sent, 0, wide)
    gate_up_sum = after(gate_up_kept, down_sent).astype(jnp.float32) + gate_up_got.astype(jnp.float32)
    joined_sum = joined_kept.astype(jnp.float32) + joined_got.astype(jnp.float32)
    down_sum = down_kept.astype(jnp.float32) + down_got.astype(jnp.float32)
    for step in range(1, wide.bit_length() - 2):
        out_sum, joined_sum, down_sum = (
            halve_again(x.astype(jnp.bfloat16), step, wide) for x in (out_sum, joined_sum, down_sum)
        )
        if step > 1:
            gate_up_sum = halve_again(gate_up_sum.astype(jnp.bfloat16), step, wide)
    gate_up_sum, down_sum, out_sum, joined_sum = gate_up_sum[0], down_sum[0], out_sum[0], joined_sum[0]
    out_sum = after(out_sum.astype(jnp.bfloat16), joined_got, down_got)
    got = swap_blocks(
        lambda j: lax.dynamic_slice_in_dim(out_sum, j * query_width, query_width, 1), here, narrow
    )
    out_sum = sum(x.astype(jnp.float32) for x in got)
    layer_out = (resid + layer_sum.astype(jnp.float32)).astype(jnp.bfloat16)
    scaled_one = normed_one_grad * attn_gain
    input_grad = back + inverse_one * (
        scaled_one - unit_one * jnp.mean(scaled_one * unit_one, axis=-1, keepdims=True)
    )
    gate_sum, up_sum = gate_up_sum[:, : w_gate.shape[1]], gate_up_sum[:, w_gate.shape[1] :]
    return (
        layer_out,
        input_grad,
        gains[0],
        gains[1],
        joined_sum[:, :query_width],
        joined_sum[:, query_width : query_width + key_width],
        joined_sum[:, query_width + key_width :],
        out_sum.T,
        gate_sum,
        up_sum,
        down_sum.T,
    )


def solution(mesh):
    in_specs = (
        P(("wide", "narrow"), None),
        P(),
        P(),
        P(None, "narrow"),
        P(None, "narrow"),
        P(None, "narrow"),
        P("narrow", None),
        P(None, "narrow"),
        P(None, "narrow"),
        P("narrow", None),
        P(("wide", "narrow"), None),
        P("wide", None),
    )
    out_specs = (
        P(("wide", "narrow"), None),
        P(("wide", "narrow"), None),
        P(),
        P(),
        P("wide", "narrow"),
        P("wide", "narrow"),
        P("wide", "narrow"),
        P("narrow", "wide"),
        P("wide", "narrow"),
        P("wide", "narrow"),
        P("narrow", "wide"),
    )
    return jax.shard_map(
        on_device, mesh=mesh, in_specs=in_specs, out_specs=out_specs, check_vma=False
    )
```

```python
import functools, math
import jax, jax.numpy as jnp
from jax import lax
from jax.experimental import pallas as pl
from jax.experimental.pallas import tpu as pltpu

from jax.sharding import PartitionSpec as P

HD = 64
EPSILON = 1e-05
THETA_BASE = 500000.0
LANES = 128
VMEM_LIMIT = 56 * 1024 * 1024
COST = pl.CostEstimate(flops=1, bytes_accessed=1, transcendentals=0)
LONG_COST = pl.CostEstimate(flops=40_000_000_000, bytes_accessed=1, transcendentals=0)


def dot_nn(a, b):
    return lax.dot_general(a, b, (((1,), (0,)), ((), ())), preferred_element_type=jnp.float32)


def dot_nt(a, b):
    return lax.dot_general(a, b, (((1,), (1,)), ((), ())), preferred_element_type=jnp.float32)


def swap_halves(x):
    parts = []
    for t in range(x.shape[1] // LANES):
        tile = x[:, t * LANES : (t + 1) * LANES]
        lane = lax.broadcasted_iota(jnp.int32, tile.shape, 1)
        left = pltpu.roll(tile, LANES - HD // 2, 1)
        right = pltpu.roll(tile, HD // 2, 1)
        parts.append(jnp.where(lane % HD < HD // 2, left, right))
    return parts[0] if len(parts) == 1 else jnp.concatenate(parts, axis=1)


def turn(x, cosine, sine):
    n = x.shape[1] // LANES
    s = swap_halves(x)
    outs = [
        x[:, i * LANES : (i + 1) * LANES] * cosine + s[:, i * LANES : (i + 1) * LANES] * sine
        for i in range(n)
    ]
    return outs[0] if n == 1 else jnp.concatenate(outs, axis=1)


def qkv_body(qw, kw, x_ref, w_ref, cos_ref, sin_ref, q_ref, k_ref, v_ref):
    y = dot_nn(x_ref[...], w_ref[...])
    c, s = cos_ref[...], sin_ref[...]
    q_ref[...] = (turn(y[:, :qw], c, s) * (HD ** -0.5)).astype(jnp.bfloat16)
    k_ref[...] = turn(y[:, qw : qw + kw], c, s).astype(jnp.bfloat16)
    v_ref[...] = y[:, qw + kw :].astype(jnp.bfloat16)


def qkv_call(x, w, cosine, sine, qw, kw):
    rows, d = x.shape
    br = min(256, rows)
    spec = lambda n: pl.BlockSpec((br, n), lambda i: (i, 0))
    return pl.pallas_call(
        functools.partial(qkv_body, qw, kw),
        grid=(rows // br,),
        in_specs=[spec(d), pl.BlockSpec(w.shape, lambda i: (0, 0)), spec(LANES), spec(LANES)],
        out_specs=[spec(qw), spec(kw), spec(kw)],
        out_shape=[
            jax.ShapeDtypeStruct((rows, qw), jnp.bfloat16),
            jax.ShapeDtypeStruct((rows, kw), jnp.bfloat16),
            jax.ShapeDtypeStruct((rows, kw), jnp.bfloat16),
        ],
        compiler_params=pltpu.CompilerParams(vmem_limit_bytes=VMEM_LIMIT),
        cost_estimate=COST,
        name="qkv",
    )(x, w, cosine, sine)


def half_mask(rows):
    lane = lax.broadcasted_iota(jnp.int32, (rows, LANES), 1)
    return lane < HD


def stack_heads(x, low):
    zero = jnp.zeros((x.shape[0], LANES), x.dtype)
    a, b = x[:, :LANES], x[:, LANES : 2 * LANES]
    return jnp.concatenate(
        [jnp.where(low, a, zero), jnp.where(low, zero, a), jnp.where(low, b, zero), jnp.where(low, zero, b)], axis=0
    )


def unstack_heads(x, low):
    r = x.shape[0] // 4
    return jnp.concatenate(
        [jnp.where(low, x[:r], x[r : 2 * r]), jnp.where(low, x[2 * r : 3 * r], x[3 * r :])], axis=1
    )


def allowed_mask(ext, b0, r, start):
    j = lax.broadcasted_iota(jnp.int32, (ext, 4 * r), 0)
    t = lax.broadcasted_iota(jnp.int32, (ext, 4 * r), 1) % r + b0
    return (j <= t) & (j >= start)


def block_extent(b0, r, total):
    return min(total, -(-(b0 + r) // LANES) * LANES)


def fwd_body(blocks, r, kv, group, q_ref, k_ref, v_ref, start_ref, o_ref, lse_ref):
    low = half_mask(r)
    total = k_ref.shape[0]
    width = group * HD
    for c in range(kv):
        vt = v_ref[:, c * LANES : (c + 1) * LANES].T
        for n, b0 in enumerate(blocks):
            ext = block_extent(b0, r, total)
            q4 = stack_heads(q_ref[b0 : b0 + r, c * width : (c + 1) * width], low)
            s = dot_nt(k_ref[:ext, c * LANES : (c + 1) * LANES], q4)
            s = jnp.where(allowed_mask(ext, b0, r, start_ref[n : n + 1, :]), s, -1e30)
            top = jnp.max(s, axis=0, keepdims=True)
            p = jnp.exp(s - top)
            total_p = jnp.sum(p, axis=0, keepdims=True)
            ot = dot_nn(vt[:, :ext], p.astype(jnp.bfloat16)) * (1.0 / total_p)
            o_ref[n * r : (n + 1) * r, c * width : (c + 1) * width] = unstack_heads(ot.T, low).astype(jnp.bfloat16)
            lse_ref[c, n : n + 1, :] = top + jnp.log(total_p)


def attend(q, k, v, start, blocks, r, kv, group):
    nb = len(blocks)
    return pl.pallas_call(
        functools.partial(fwd_body, blocks, r, kv, group),
        out_shape=[
            jax.ShapeDtypeStruct((nb * r, kv * group * HD), jnp.bfloat16),
            jax.ShapeDtypeStruct((kv, nb, 4 * r), jnp.float32),
        ],
        compiler_params=pltpu.CompilerParams(vmem_limit_bytes=VMEM_LIMIT),
        cost_estimate=COST,
        name="attend",
    )(q, k, v, start)


def bwd_body(blocks, r, kv, group, first, last, *refs):
    refs = list(refs)
    q_ref, k_ref, v_ref, start_ref, do_ref, o_ref, lse_ref = refs[:7]
    refs = refs[7:]
    if not first:
        dq_in, dk_in, dv_in = refs[:3]
        refs = refs[3:]
    if last:
        cos_ref, sin_ref = refs[:2]
        out_ref, dq_s, dk_s, dv_s = refs[2:]
    else:
        dq_s, dk_s, dv_s = refs
    low = half_mask(r)
    total = k_ref.shape[0]
    width = group * HD
    for c in range(kv):
        cl = slice(c * LANES, (c + 1) * LANES)
        cw = slice(c * width, (c + 1) * width)
        kt = k_ref[:, cl].T
        if first:
            dk_s[:, cl] = jnp.zeros((total, LANES), jnp.float32)
            dv_s[:, cl] = jnp.zeros((total, LANES), jnp.float32)
        else:
            dk_s[:, cl] = dk_in[:, cl]
            dv_s[:, cl] = dv_in[:, cl]
        for n, b0 in enumerate(blocks):
            ext = block_extent(b0, r, total)
            q4 = stack_heads(q_ref[b0 : b0 + r, cw], low)
            do4 = stack_heads(do_ref[n * r : (n + 1) * r, cw], low)
            o4 = stack_heads(o_ref[n * r : (n + 1) * r, cw], low)
            delta = jnp.sum((do4.astype(jnp.float32) * o4.astype(jnp.float32)).T, axis=0, keepdims=True)
            s = dot_nt(k_ref[:ext, cl], q4)
            p = jnp.exp(
                jnp.where(allowed_mask(ext, b0, r, start_ref[n : n + 1, :]), s - lse_ref[c, n : n + 1, :], -1e30)
            )
            dp = dot_nt(v_ref[:ext, cl], do4)
            ds = (p * (dp - delta)).astype(jnp.bfloat16)
            dq4 = dot_nn(kt[:, :ext], ds).T
            dq_s[n * r : (n + 1) * r, cw] = unstack_heads(dq4, low) * (HD ** -0.5)
            dk_s[:ext, cl] += dot_nn(ds, q4)
            dv_s[:ext, cl] += dot_nn(p.astype(jnp.bfloat16), do4)
    if not last:
        return
    nc = 1 if first else 2
    cosine, sine = cos_ref[...], -sin_ref[...]
    qw = kv * width
    for n, b0 in enumerate(blocks):
        cs, sn = cos_ref[b0 : b0 + r, :], -sin_ref[b0 : b0 + r, :]
        out_ref[b0 : b0 + r, :qw] = turn(dq_s[n * r : (n + 1) * r, :], cs, sn).astype(jnp.bfloat16)
        if not first:
            a0 = b0 - r
            cs, sn = cos_ref[a0 : a0 + r, :], -sin_ref[a0 : a0 + r, :]
            out_ref[a0 : a0 + r, :qw] = turn(dq_in[n * r : (n + 1) * r, :], cs, sn).astype(jnp.bfloat16)
    lane = lax.broadcasted_iota(jnp.int32, (total, LANES), 1) < HD

    def fold(x):
        return x + pltpu.roll(x, HD, 1)

    for i, (ref, rot) in enumerate(((dk_s, True), (dv_s, False))):
        for c in range(0, kv, 2):
            x = fold(ref[:, c * LANES : (c + 1) * LANES])
            if c + 1 < kv:
                x = jnp.where(lane, x, fold(ref[:, (c + 1) * LANES : (c + 2) * LANES]))
            if rot:
                x = turn(x, cosine, sine)
            x = x.astype(jnp.bfloat16)
            at = qw + i * kv * HD + c * HD
            if c + 1 < kv:
                out_ref[:, at : at + LANES] = x
            else:
                out_ref[:, at : at + HD] = x[:, :HD]


def attend_back(q, k, v, start, do, o, lse, carried, tables, blocks, r, kv, group):
    first, last = carried is None, tables is not None
    rows = q.shape[0]
    nb = len(blocks)
    sums = [
        jax.ShapeDtypeStruct((nb * r, kv * group * HD), jnp.float32),
        jax.ShapeDtypeStruct((rows, kv * LANES), jnp.float32),
        jax.ShapeDtypeStruct((rows, kv * LANES), jnp.float32),
    ]
    if last:
        out = jax.ShapeDtypeStruct((rows, kv * (group + 2) * HD), jnp.bfloat16)
        scratch = [pltpu.VMEM(s.shape, s.dtype) for s in sums]
    else:
        out, scratch = sums, []
    args = (q, k, v, start, do, o, lse) + (() if first else tuple(carried)) + (tuple(tables) if last else ())
    return pl.pallas_call(
        functools.partial(bwd_body, blocks, r, kv, group, first, last),
        out_shape=out,
        scratch_shapes=scratch,
        compiler_params=pltpu.CompilerParams(vmem_limit_bytes=VMEM_LIMIT),
        cost_estimate=LONG_COST,
        name="attend_back",
    )(*args)


def grad_body(nl, nr, got, tiles_ref, *refs):
    lefts = refs[:nl]
    rights = [refs[nl + i * nl : nl + (i + 1) * nl] for i in range(nr)]
    refs = refs[nl + nl * nr :]
    recv, outs = (refs[0], refs[1:]) if got else (None, refs)
    half = pl.num_programs(0) // 2
    step = pl.program_id(0)
    turned = [x[...].T for x in lefts]
    at = 0
    for right in rights:
        total = dot_nn(turned[0], right[0][...])
        for a, b in zip(turned[1:], right[1:]):
            total += dot_nn(a, b[...])
        here = slice(at, at + total.shape[1])
        at += total.shape[1]
        if not got:
            outs[0][0, :, here] = total.astype(jnp.bfloat16)
            continue
        total = (total + recv[0, :, here].astype(jnp.float32)).astype(jnp.bfloat16)

        @pl.when(step < half)
        def _():
            outs[0][0, :, here] = total

        @pl.when(step >= half)
        def _():
            outs[1][0, :, here] = total


def grad_call(tiles, part, lefts, rights, recv=None):
    count = tiles.shape[0]
    half = count // 2
    nl, nr = len(lefts), len(rights)
    cols = sum(r[0].shape[1] for r in rights)
    got = recv is not None
    shift = half if got else 0
    in_specs = [pl.BlockSpec((x.shape[0], part), lambda j, t: (0, t[lax.rem(j + shift, count)])) for x in lefts]
    in_specs += [
        pl.BlockSpec(x.shape, lambda j, t: (0, 0), pipeline_mode=pl.Buffered(1)) for r in rights for x in r
    ]
    if got:
        in_specs.append(pl.BlockSpec((1, part, cols), lambda j, t: (lax.rem(j + shift, count), 0, 0)))
        out_specs = [
            pl.BlockSpec((1, part, cols), lambda j, t: (jnp.minimum(j, half - 1), 0, 0)),
            pl.BlockSpec((1, part, cols), lambda j, t: (jnp.maximum(j - half, 0), 0, 0)),
        ]
        out_shape = [jax.ShapeDtypeStruct((half, part, cols), jnp.bfloat16)] * 2
    else:
        out_specs = pl.BlockSpec((1, part, cols), lambda j, t: (j, 0, 0))
        out_shape = jax.ShapeDtypeStruct((count, part, cols), jnp.bfloat16)
    return pl.pallas_call(
        functools.partial(grad_body, nl, nr, got),
        grid_spec=pltpu.PrefetchScalarGridSpec(
            num_scalar_prefetch=1, grid=(count,), in_specs=in_specs, out_specs=out_specs
        ),
        out_shape=out_shape,
        compiler_params=pltpu.CompilerParams(vmem_limit_bytes=VMEM_LIMIT),
        cost_estimate=COST,
        name="weight_grad",
    )(tiles, *lefts, *[x for r in rights for x in r], *((recv,) if got else ()))


def place(index, part):
    return pl.ds(pl.multiple_of(index * part, part), part)


def out_body(at_ref, x_ref, *refs):
    pieces, out = refs[:-1], refs[-1]
    x = jnp.concatenate([x_ref[j] for j in range(x_ref.shape[0])], axis=1)
    for n, piece in enumerate(pieces):
        out[:, place(at_ref[n], piece.shape[1])] = dot_nn(x, piece[...])


def out_project(at, x, pieces):
    rows, width = x.shape[1], len(pieces) * pieces[0].shape[1]
    return pl.pallas_call(
        out_body,
        in_specs=[pl.BlockSpec(memory_space=pltpu.SMEM)] + [pl.BlockSpec(memory_space=pltpu.VMEM)] * (1 + len(pieces)),
        out_specs=pl.BlockSpec(memory_space=pltpu.VMEM),
        out_shape=jax.ShapeDtypeStruct((rows, width), jnp.float32),
        compiler_params=pltpu.CompilerParams(vmem_limit_bytes=VMEM_LIMIT),
        cost_estimate=COST,
        name="out_project",
    )(at, x, *pieces)


def out_back_body(at_ref, x_ref, *refs):
    pieces, out = refs[:-1], refs[-1]
    total = None
    for n, piece in enumerate(pieces):
        term = dot_nt(x_ref[:, place(at_ref[n], piece.shape[1])], piece[...])
        total = term if total is None else total + term
    total = total.astype(jnp.bfloat16)
    width = out.shape[2]
    for j in range(out.shape[0]):
        out[j] = total[:, j * width : (j + 1) * width]


def out_project_back(at, x, pieces, parts):
    rows, depth = x.shape[0], pieces[0].shape[0]
    return pl.pallas_call(
        out_back_body,
        in_specs=[pl.BlockSpec(memory_space=pltpu.SMEM)] + [pl.BlockSpec(memory_space=pltpu.VMEM)] * (1 + len(pieces)),
        out_specs=pl.BlockSpec(memory_space=pltpu.VMEM),
        out_shape=jax.ShapeDtypeStruct((parts, rows, depth // parts), jnp.bfloat16),
        compiler_params=pltpu.CompilerParams(vmem_limit_bytes=VMEM_LIMIT),
        cost_estimate=COST,
        name="out_project_back",
    )(at, x, *pieces)


def in_back_body(at_ref, x_ref, *refs):
    pieces, out = refs[:-1], refs[-1]
    x = x_ref[...]
    for n, piece in enumerate(pieces):
        out[:, place(at_ref[n], piece.shape[0])] = dot_nt(x, piece[...])


def in_project_back(at, x, pieces):
    rows, width = x.shape[0], len(pieces) * pieces[0].shape[0]
    return pl.pallas_call(
        in_back_body,
        in_specs=[pl.BlockSpec(memory_space=pltpu.SMEM)] + [pl.BlockSpec(memory_space=pltpu.VMEM)] * (1 + len(pieces)),
        out_specs=pl.BlockSpec(memory_space=pltpu.VMEM),
        out_shape=jax.ShapeDtypeStruct((rows, width), jnp.float32),
        compiler_params=pltpu.CompilerParams(vmem_limit_bytes=VMEM_LIMIT),
        cost_estimate=COST,
        name="in_project_back",
    )(at, x, *pieces)


def mlp_body(x_ref, dy_ref, wg_ref, wu_ref, wd_ref, m_ref, dg_ref, du_ref):
    x, dy = x_ref[...], dy_ref[...]
    gate = dot_nn(x, wg_ref[...])
    up = dot_nn(x, wu_ref[...])
    dm = dot_nt(dy, wd_ref[...])
    sig = 1.0 / (1.0 + jnp.exp(-gate))
    act = gate * sig
    m_ref[...] = (act * up).astype(jnp.bfloat16)
    du_ref[...] = (dm * act).astype(jnp.bfloat16)
    dg_ref[...] = (dm * up * (sig * (1.0 + gate * (1.0 - sig)))).astype(jnp.bfloat16)


def mlp_call(x, dy, wg, wu, wd):
    t, d = x.shape
    f = wg.shape[1]
    bf = min(256, f)
    col = pl.BlockSpec((d, bf), lambda i: (0, i))
    hid = pl.BlockSpec((t, bf), lambda i: (0, i))
    held = pl.BlockSpec((t, d), lambda i: (0, 0), pipeline_mode=pl.Buffered(1))
    return pl.pallas_call(
        mlp_body,
        grid=(f // bf,),
        in_specs=[held, held, col, col, pl.BlockSpec((bf, d), lambda i: (i, 0))],
        out_specs=[hid] * 3,
        out_shape=[jax.ShapeDtypeStruct((t, f), jnp.bfloat16)] * 3,
        compiler_params=pltpu.CompilerParams(vmem_limit_bytes=VMEM_LIMIT),
        cost_estimate=COST,
        name="mlp",
    )(x, dy, wg, wu, wd)


def mlp_back_body(dg_ref, du_ref, wg_ref, wu_ref, o_ref):
    o_ref[...] = (dot_nt(dg_ref[...], wg_ref[...]) + dot_nt(du_ref[...], wu_ref[...])).astype(jnp.bfloat16)


def mlp_back_call(dg, du, wg, wu):
    t, f = dg.shape
    d = wg.shape[0]
    bn = min(512, d)
    held = pl.BlockSpec((t, f), lambda i: (0, 0), pipeline_mode=pl.Buffered(1))
    row = pl.BlockSpec((bn, f), lambda i: (i, 0))
    return pl.pallas_call(
        mlp_back_body,
        grid=(d // bn,),
        in_specs=[held, held, row, row],
        out_specs=pl.BlockSpec((t, bn), lambda i: (0, i)),
        out_shape=jax.ShapeDtypeStruct((t, d), jnp.bfloat16),
        compiler_params=pltpu.CompilerParams(vmem_limit_bytes=VMEM_LIMIT),
        cost_estimate=COST,
        name="mlp_back",
    )(dg, du, wg, wu)


def mat_body(transposed, x_ref, w_ref, o_ref):
    o_ref[...] = (dot_nt if transposed else dot_nn)(x_ref[...], w_ref[...]).astype(jnp.bfloat16)


def mat_call(x, w, transposed):
    rows, depth = x.shape
    width = w.shape[0] if transposed else w.shape[1]
    bn = min(512, width)
    w_spec = pl.BlockSpec((bn, depth), lambda i: (i, 0)) if transposed else pl.BlockSpec((depth, bn), lambda i: (0, i))
    return pl.pallas_call(
        functools.partial(mat_body, transposed),
        grid=(width // bn,),
        in_specs=[pl.BlockSpec((rows, depth), lambda i: (0, 0), pipeline_mode=pl.Buffered(1)), w_spec],
        out_specs=pl.BlockSpec((rows, bn), lambda i: (0, i)),
        out_shape=jax.ShapeDtypeStruct((rows, width), jnp.bfloat16),
        compiler_params=pltpu.CompilerParams(vmem_limit_bytes=VMEM_LIMIT),
        cost_estimate=COST,
        name="product",
    )(x, w)


def down_body(x_ref, w_ref, *refs):
    out = refs[-1]
    out[...] = dot_nn(x_ref[...], w_ref[...]).astype(jnp.bfloat16).reshape(out.shape)


def down_call(x, w, blocks, chunks, chunk, into=None):
    rows, depth = x.shape
    width = w.shape[1]
    bn = min(512, width)
    r = rows // blocks
    return pl.pallas_call(
        down_body,
        grid=(width // bn,),
        in_specs=[
            pl.BlockSpec((rows, depth), lambda i: (0, 0), pipeline_mode=pl.Buffered(1)),
            pl.BlockSpec((depth, bn), lambda i: (0, i)),
        ] + ([] if into is None else [pl.BlockSpec(memory_space=pl.ANY)]),
        out_specs=pl.BlockSpec((blocks, 1, r, bn), lambda i: (0, chunk, 0, i)),
        out_shape=jax.ShapeDtypeStruct((blocks, chunks, r, width), jnp.bfloat16),
        input_output_aliases={} if into is None else {2: 0},
        compiler_params=pltpu.CompilerParams(vmem_limit_bytes=VMEM_LIMIT),
        cost_estimate=COST,
        name="down",
    )(x, w, *(() if into is None else (into,)))


def doc_layout(lengths, total_rows):
    ends = jnp.cumsum(lengths)
    starts = ends - lengths
    places = jnp.arange(total_rows, dtype=jnp.int32)
    owner = jnp.sum((places[:, None] >= ends[None, :]).astype(jnp.int32), axis=1)
    picked = owner[:, None] == jnp.arange(lengths.shape[0], dtype=jnp.int32)[None, :]
    first = jnp.sum(jnp.where(picked, starts[None, :], 0), axis=1)
    return first, (places - first).astype(jnp.float32)


def angle_tables(positions):
    indices = jnp.arange(HD // 2, dtype=jnp.float32)
    inverse = jnp.exp(indices * (-2.0 * math.log(THETA_BASE) / HD))
    turned = positions[:, None] * inverse[None, :]
    cosine, sine = jnp.cos(turned), jnp.sin(turned)
    return (
        jnp.concatenate([cosine] * 4, axis=1),
        jnp.concatenate([-sine, sine, -sine, sine], axis=1),
    )


def twice(w):
    heads = w.shape[1] // HD
    return jnp.concatenate([w[:, i * HD : (i + 1) * HD] for i in range(heads) for _ in range(2)], axis=1)


def after(value, *others):
    return lax.optimization_barrier((value, *others))[0]


def scatter_direct(parts, index, size):
    def block(at):
        return lax.dynamic_index_in_dim(parts, at, 0, keepdims=False)

    total = block(index).astype(jnp.float32)
    for k in range(1, size):
        got = lax.ppermute(block(index ^ k), "narrow", [(i, i ^ k) for i in range(size)])
        total = total + got.astype(jnp.float32)
    return total


def swap_blocks(block, index, size):
    return [block(index)] + [
        lax.ppermute(block(index ^ k), "narrow", [(i, i ^ k) for i in range(size)]) for k in range(1, size)
    ]


def in_order(items, index):
    step = 1
    while step < len(items):
        flip = (index & step) != 0
        items = [jnp.where(flip, items[k ^ step], items[k]) for k in range(len(items))]
        step *= 2
    return items


def high_bits(size):
    first = list(range(1, size.bit_length() - 1))
    return first, first[::-1]


def by_core(size, step):
    bits = high_bits(size)
    return [(i, i ^ (1 << bits[i & 1][step])) for i in range(size)]


def masks(size):
    both = []
    for bits in high_bits(size):
        out = [0]
        for bit in bits[::-1]:
            out = out + [o ^ (1 << bit) for o in out]
        both.append(jnp.array(out, dtype=jnp.int32))
    return both


def gather_plane(piece, size):
    pieces = [piece]
    for step in range(size.bit_length() - 2)[::-1]:
        pieces = pieces + [lax.ppermute(p, "wide", by_core(size, step)) for p in pieces]
    return pieces


def gather_cores(pieces, index, size):
    even, odd = masks(size)
    first = (index & 1) == 0
    pieces = pieces + [lax.ppermute(p, "wide", [(i, i ^ 1) for i in range(size)]) for p in pieces]
    owners = jnp.concatenate([index ^ jnp.where(first, even, odd), index ^ 1 ^ jnp.where(first, odd, even)])
    return pieces, owners.astype(jnp.int32)


def scatter_narrow(parts):
    return lax.psum_scatter(parts, "narrow", scatter_dimension=0, tiled=True)


def grads_sent(lefts, rights, index, size):
    even, odd = masks(size)
    part = lefts[0].shape[1] // size
    tiles = (index ^ 1 ^ jnp.where((index & 1) == 0, odd, even)).astype(jnp.int32)
    return grad_call(tiles, part, lefts, rights)


def swap_cores(sent, size):
    return lax.ppermute(sent, "wide", [(i, i ^ 1) for i in range(size)])


def grads_kept(lefts, rights, got, index, size):
    even, odd = masks(size)
    part = lefts[0].shape[1] // size
    tiles = (index ^ jnp.where((index & 1) == 0, even, odd)).astype(jnp.int32)
    return grad_call(tiles, part, lefts, rights, got)


def swap_plane(sent, step, size):
    return lax.ppermute(sent, "wide", by_core(size, step))


def halve(sent, kept, step, size):
    return kept.astype(jnp.float32) + swap_plane(sent, step, size).astype(jnp.float32)


def halve_again(value, step, size):
    half = value.shape[0] // 2
    return halve(value[half:], value[:half], step, size)


def sum_plane(array, size):
    items = [array] + [
        lax.ppermute(array, "wide", [(i, i ^ (2 * flip)) for i in range(size)]) for flip in range(1, size // 2)
    ]
    return sum(in_order(items, lax.axis_index("wide") >> 1))


def sum_column(array, narrow, size):
    array = array + lax.ppermute(array, "wide", [(i, i ^ 1) for i in range(size)])
    for bit in range(narrow.bit_length() - 1):
        array = array + lax.ppermute(array, "narrow", [(i, i ^ (1 << bit)) for i in range(narrow)])
    return array


def on_device(
    hidden_in, attn_gain, mlp_gain, w_query, w_key, w_value, w_out, w_gate, w_up, w_down, upstream, doc_lengths
):
    narrow, wide = lax.axis_size("narrow"), lax.axis_size("wide")
    here, wide_here = lax.axis_index("narrow"), lax.axis_index("wide")
    local_rows, width = hidden_in.shape
    total_rows = local_rows * narrow
    chunks = 2
    r = local_rows // chunks
    query_width, key_width = w_query.shape[1], w_key.shape[1]
    kv = key_width // HD
    group = query_width // key_width
    first, positions = doc_layout(doc_lengths[0], total_rows)
    tables = angle_tables(positions)
    start = jnp.tile(first.astype(jnp.int32).reshape(narrow, local_rows), (1, 4))
    blocks = [z * local_rows for z in range(narrow)]
    w_twice = jnp.concatenate([w_query, twice(w_key), twice(w_value)], axis=1)
    w_joined = jnp.concatenate([w_query, w_key, w_value], axis=1)
    part = width // wide

    source = hidden_in.astype(jnp.float32)
    inverse_one = lax.rsqrt(jnp.mean(source * source, axis=-1, keepdims=True) + EPSILON)
    unit_one = source * inverse_one
    normed_one = (unit_one * attn_gain).astype(jnp.bfloat16)
    full_one = lax.all_gather(normed_one, "narrow", axis=0, tiled=True)

    w_out_part = lax.dynamic_slice_in_dim(w_out, wide_here * part, part, 1)
    w_out_part = jnp.concatenate(
        in_order(swap_blocks(lambda j: w_out_part, here, narrow), here), axis=0
    )
    w_out_plane = gather_plane(w_out_part, wide)
    full_one, w_twice, tables, w_out_plane = lax.optimization_barrier((full_one, w_twice, tables, w_out_plane))
    w_out_parts, w_out_at = gather_cores(w_out_plane, wide_here, wide)

    dy_a = lax.all_gather(after(upstream[:r], full_one), "narrow", axis=0, tiled=True)
    q, k, v = qkv_call(full_one, w_twice, *tables, query_width, 2 * key_width)

    def swap_heads(x):
        return lax.all_to_all(x.reshape(total_rows, query_width), "narrow", 0, 0, tiled=True)

    def second_norm(summed):
        resid = source + summed
        inverse = lax.rsqrt(jnp.mean(resid * resid, axis=-1, keepdims=True) + EPSILON)
        unit = resid * inverse
        return resid, inverse, unit, (unit * mlp_gain).astype(jnp.bfloat16)

    heads, lse = attend(q, k, v, start, blocks, local_rows, kv, group)
    heads_rows = swap_heads(heads).reshape(narrow, local_rows, query_width)
    dy_b = lax.all_gather(after(upstream[r:], heads_rows), "narrow", axis=0, tiled=True)
    resid, inverse_two, unit_two, normed_two = second_norm(
        out_project(w_out_at, after(heads_rows, dy_a), w_out_parts)
    )
    normed_a, normed_b, dy_b = lax.optimization_barrier((normed_two[:r], normed_two[r:], dy_b))
    full_a = lax.all_gather(normed_a, "narrow", axis=0, tiled=True)
    full_b = lax.all_gather(after(normed_b, full_a), "narrow", axis=0, tiled=True)

    m_a, dg_a, du_a = mlp_call(full_a, dy_a, w_gate, w_up, w_down)
    parts_a = mlp_back_call(dg_a, du_a, w_gate, w_up)
    grad_a = scatter_narrow(parts_a)
    y_a = down_call(after(m_a, parts_a), w_down, narrow, chunks, 0)
    m_b, dg_b, du_b = mlp_call(full_b, after(dy_b, y_a), w_gate, w_up, w_down)
    parts_b = mlp_back_call(dg_b, du_b, w_gate, w_up)
    parts_b, grad_a = lax.optimization_barrier((parts_b, grad_a))
    grad_b = scatter_narrow(parts_b)

    here_wide = (wide_here, wide)
    gate_up = [full_a, after(full_b, parts_b)], [[dg_a, dg_b], [du_a, du_b]]
    sent_gate_up = grads_sent(*gate_up, *here_wide)
    down = [after(dy_a, sent_gate_up), dy_b], [[m_a, m_b]]
    sent_down = grads_sent(*down, *here_wide)
    y = down_call(after(m_b, sent_down), w_down, narrow, chunks, 1, y_a)
    layer_sum = scatter_narrow(after(y, grad_b).reshape(total_rows, width))
    unit_late = after(unit_two, y)
    grad_a, grad_b = grad_a.astype(jnp.float32), grad_b.astype(jnp.float32)
    scaled_grad = jnp.concatenate([grad_a, grad_b], axis=0)
    scaled = scaled_grad * mlp_gain
    back = upstream.astype(jnp.float32) + inverse_two * (
        scaled - unit_late * jnp.mean(scaled * unit_late, axis=-1, keepdims=True)
    )
    gain_two = jnp.sum(scaled_grad * unit_late, axis=0)
    low = back.astype(jnp.bfloat16)
    heads_grad = out_project_back(w_out_at, low, w_out_parts, narrow)
    got_gate_up = swap_cores(after(sent_gate_up, low), wide)
    got_down = swap_cores(after(sent_down, low), wide)
    gate_up = [after(full_a, heads_grad), full_b], gate_up[1]
    gate_up_sent, gate_up_kept = grads_kept(*gate_up, got_gate_up, *here_wide)
    down = [after(dy_a, gate_up_sent), dy_b], [[m_a, m_b]]
    down_sent, down_kept = grads_kept(*down, got_down, *here_wide)
    heads_side = jnp.concatenate([heads_rows[j] for j in range(narrow)], axis=1)
    heads_grad = swap_heads(heads_grad)
    joined_grad = attend_back(
        after(q, down_sent), k, v, start, heads_grad, heads, lse, None, tables, blocks, local_rows, kv, group
    )
    gate_up_got = swap_plane(gate_up_sent, 0, wide)
    down_got = swap_plane(down_sent, 0, wide)

    def halved(kept, got):
        out = (kept.astype(jnp.float32) + got.astype(jnp.float32)).astype(jnp.bfloat16)
        return out[: out.shape[0] // 2], out[out.shape[0] // 2 :]

    parts = mat_call(joined_grad, after(w_joined, layer_sum), True)
    normed_one_grad = scatter_narrow(parts).astype(jnp.float32)
    out = [after(low, parts, gate_up_got, down_got)], [[heads_side]]
    sent_out = grads_sent(*out, *here_wide)
    gate_up_kept, gate_up_sent = halved(gate_up_kept, gate_up_got)
    gate_up_got = swap_plane(gate_up_sent, 1, wide)
    joined = [after(full_one, sent_out)], [[joined_grad]]
    sent_joined = grads_sent(*joined, *here_wide)
    out = [after(low, sent_joined)], [[heads_side]]
    out_sent, out_kept = grads_kept(*out, swap_cores(sent_out, wide), *here_wide)
    down_kept, down_sent = halved(down_kept, down_got)
    down_got = swap_plane(down_sent, 1, wide)
    joined = [after(full_one, out_sent)], [[joined_grad]]
    joined_sent, joined_kept = grads_kept(*joined, swap_cores(sent_joined, wide), *here_wide)
    parts_late, _ = lax.optimization_barrier((parts, joined_sent))
    gain_one = jnp.sum(parts_late.astype(jnp.float32) * full_one.astype(jnp.float32), axis=0) / attn_gain
    gains = sum_column(sum_plane(jnp.stack([gain_one, gain_two]), wide), narrow, wide)
    gate_up_sum = after(gate_up_kept, joined_sent).astype(jnp.float32) + gate_up_got.astype(jnp.float32)
    down_sum = after(down_kept, joined_sent).astype(jnp.float32) + down_got.astype(jnp.float32)
    joined_got = swap_plane(joined_sent, 0, wide)
    out_got = swap_plane(out_sent, 0, wide)
    joined_sum = joined_kept.astype(jnp.float32) + joined_got.astype(jnp.float32)
    out_sum = out_kept.astype(jnp.float32) + out_got.astype(jnp.float32)
    for step in range(1, wide.bit_length() - 2):
        out_sum, joined_sum = (halve_again(x.astype(jnp.bfloat16), step, wide) for x in (out_sum, joined_sum))
        if step > 1:
            gate_up_sum, down_sum = (
                halve_again(x.astype(jnp.bfloat16), step, wide) for x in (gate_up_sum, down_sum)
            )
    gate_up_sum, down_sum, out_sum, joined_sum = gate_up_sum[0], down_sum[0], out_sum[0], joined_sum[0]
    out_sum = out_sum.astype(jnp.bfloat16)
    got = swap_blocks(
        lambda j: lax.dynamic_slice_in_dim(out_sum, j * query_width, query_width, 1), here, narrow
    )
    out_sum = sum(x.astype(jnp.float32) for x in got)
    layer_out = (resid + layer_sum.astype(jnp.float32)).astype(jnp.bfloat16)
    scaled_one = normed_one_grad * attn_gain
    input_grad = back + inverse_one * (
        scaled_one - unit_one * jnp.mean(scaled_one * unit_one, axis=-1, keepdims=True)
    )
    gate_sum, up_sum = gate_up_sum[:, : w_gate.shape[1]], gate_up_sum[:, w_gate.shape[1] :]
    return (
        layer_out,
        input_grad,
        gains[0],
        gains[1],
        joined_sum[:, :query_width],
        joined_sum[:, query_width : query_width + key_width],
        joined_sum[:, query_width + key_width :],
        out_sum.T,
        gate_sum,
        up_sum,
        down_sum.T,
    )


def solution(mesh):
    in_specs = (
        P(("wide", "narrow"), None),
        P(),
        P(),
        P(None, "narrow"),
        P(None, "narrow"),
        P(None, "narrow"),
        P("narrow", None),
        P(None, "narrow"),
        P(None, "narrow"),
        P("narrow", None),
        P(("wide", "narrow"), None),
        P("wide", None),
    )
    out_specs = (
        P(("wide", "narrow"), None),
        P(("wide", "narrow"), None),
        P(),
        P(),
        P("wide", "narrow"),
        P("wide", "narrow"),
        P("wide", "narrow"),
        P("narrow", "wide"),
        P("wide", "narrow"),
        P("wide", "narrow"),
        P("narrow", "wide"),
    )
    return jax.shard_map(
        on_device, mesh=mesh, in_specs=in_specs, out_specs=out_specs, check_vma=False
    )
```
